32 devices in a mesh: req: 8 (over z, y), tp: 4 (over x, core).
Axes of the slice: x: 2, y: 2, z: 4, core: 2. Of those that a mesh axis runs over, the one named last changes fastest.
Arguments:
- queries: bfloat16 [3072, 2048], P('req', 'tp'), may hold values from -32 to 32
- tree_kv: bfloat16 [3072, 256], P('req'), may hold values from -6 to 6
- suffix_kv: bfloat16 [48, 256, 256], P('req'), may hold values from -6 to 6
- suffix_len: int32 [48], P('req'), may hold values from 1 to 256
- group_ids: int32 [48], P('req'), may hold values from 0 to 1
- parents: int32 [48, 64], P('req'), may hold values from 0 to 62, as said below
- accepted: int32 [48, 8], P('req'), may hold values from 0 to 63, as said below
- prompt_kv: bfloat16 [2, 256, 256], P(None, 'req'), may hold values from -12 to 12
- out_weight: bfloat16 [2048, 2048], P('tp'), may hold values from -0.5 to 0.5
Outputs:
- layer_output: bfloat16 [3072, 2048], P(('req', 'tp'))
- path_cache: bfloat16 [48, 8, 256], P('req')
The draws below stay inside these ranges and needn't reach their ends.
Inputs may be any that keep to these rules, and one draw needn't show every extreme that they name: parents[r, 0] = 0 and parents[r, i] < i for i >= 1, so node 0 is every tree's root. accepted[r] runs from the root down one branch: accepted[r, 0] = 0 and accepted[r, t - 1] = parents[r, accepted[r, t]].
All inputs are finite; a program needn't handle non-finite values.
Results may differ from the reference program's by a relative error of at most 0.017.
Values may be sent and summed in bfloat16 or wider, within the bound.
No kernel may reach another device: no remote copies, remote signals or barrier semaphores. Data moves between devices by JAX's collectives and lax.ppermute only.
A program may use at most 64 MiB of HBM per device.

```python
import jax
import jax.numpy as jnp
from jax import lax

D = 2048
HEADS = 16
HD = 128
REQ_DEV = 6
TREE = 64
PATH = 8
SUF = 256
NGROUPS = 2
REQS = 48
TOKENS = 3072
PROMPT = 256


def tree_helper(key):
    base = jax.random.fold_in(key, 5)
    first, second, third = jax.random.split(base, 3)
    steps = jax.random.randint(first, (REQS, TREE), 1, 5, dtype=jnp.int32)
    positions = jnp.arange(TREE, dtype=jnp.int32)
    parents = jnp.maximum(positions[None, :] - steps, 0)
    stride_top = max(1, (TREE - 1) // (PATH - 1))
    strides = jax.random.randint(second, (REQS, PATH - 1), 1, stride_top + 1, dtype=jnp.int32)
    nodes = jnp.concatenate([jnp.zeros((REQS, 1), jnp.int32), jnp.cumsum(strides, axis=1).astype(jnp.int32)], axis=1)
    forced = jax.random.randint(third, (), 0, REQS, dtype=jnp.int32)
    rows = jnp.arange(REQS, dtype=jnp.int32)
    last = jnp.where(rows == forced, TREE - 1, nodes[:, PATH - 1])
    accepted = jnp.concatenate([nodes[:, :PATH - 1], last[:, None]], axis=1)
    row_index = jnp.broadcast_to(rows[:, None], (REQS, PATH - 1))
    parents = parents.at[row_index, accepted[:, 1:]].set(accepted[:, :-1])
    return (parents, accepted)


def draw_parents(key, part):
    return tree_helper(key)[0]


def draw_accepted(key, part):
    return tree_helper(key)[1]


def draw_suffix_len(key, part):
    base = jax.random.fold_in(key, 11)
    first, second, third, fourth = jax.random.split(base, 4)
    device_count = REQS // REQ_DEV
    caps = jax.random.randint(first, (device_count,), max(1, SUF // 4), SUF + 1, dtype=jnp.int32)
    full_device = jax.random.randint(second, (), 0, device_count, dtype=jnp.int32)
    caps = jnp.where(jnp.arange(device_count, dtype=jnp.int32) == full_device, SUF, caps)
    raw = jax.random.randint(third, (device_count, REQ_DEV), 0, 1 << 20, dtype=jnp.int32) % caps[:, None] + 1
    full_slot = jax.random.randint(fourth, (device_count,), 0, REQ_DEV, dtype=jnp.int32)
    lengths = jnp.where(jnp.arange(REQ_DEV, dtype=jnp.int32)[None, :] == full_slot[:, None], caps[:, None], raw)
    return lengths.reshape(REQS)


def draw_queries(key, part):
    base = jax.random.fold_in(key, 21)
    return jnp.clip(2.0 * jax.random.normal(base, (TOKENS, D), jnp.float32), -12.0, 12.0).astype(jnp.bfloat16)


def draw_prompt_kv(key, part):
    base = jax.random.fold_in(key, 31)
    first = jax.random.fold_in(base, 0)
    shape = (NGROUPS, PROMPT, 2 * HD)
    return jnp.clip(jax.random.normal(first, shape, jnp.float32), -6.0, 6.0).astype(jnp.bfloat16)


def with_ends(array, rng, low, top_value):
    longest = array.shape.index(max(array.shape))
    spots = []
    for shift in (0, 1):
        where = [jax.random.randint(jax.random.fold_in(rng, axis), (), 0, length) for axis, length in enumerate(array.shape)]
        where[longest] = (where[longest] + shift) % array.shape[longest]
        spots.append(tuple(where))
    return array.at[spots[0]].set(low).at[spots[1]].set(top_value)


def levels(own_key, shape, shards, smallest, top_value):
    level = 1.0
    for dim, blocks in shards:
        heights = jax.random.uniform(jax.random.fold_in(jax.random.fold_in(own_key, 6), dim), (blocks,), jnp.float32, smallest / len(shards), top_value / len(shards))
        level = level * jnp.repeat(jnp.exp(heights), shape[dim] // blocks).reshape((-1,) + (1,) * (len(shape) - 1 - dim))
    return level


def gaussian(key, dims, deviation, limit, shards=(), held_as=jnp.bfloat16):
    entries = deviation * jax.random.normal(key, dims, jnp.float32)
    if shards:
        entries = entries * levels(key, dims, shards, -0.22, 0.18)
    return jnp.clip(entries, -limit, limit).astype(held_as)


def setup_inputs(seed: int = 0) -> dict:
    splits = jax.random.split(jax.random.key(seed), 10)
    return {
        "queries": draw_queries(jax.random.fold_in(splits[9], 71), 0),
        "tree_kv": gaussian(splits[1], (TOKENS, 2 * HD), 1.0, 6.0, ((0, 8),)),
        "suffix_kv": gaussian(splits[2], (REQS, SUF, 2 * HD), 1.0, 6.0, ((0, 8),)),
        "suffix_len": draw_suffix_len(jax.random.fold_in(splits[9], 71), 0),
        "group_ids": with_ends(jax.random.randint(splits[4], (REQS,), 0, NGROUPS), jax.random.fold_in(splits[4], 1), 0, NGROUPS - 1).astype(jnp.int32),
        "parents": draw_parents(jax.random.fold_in(splits[9], 71), 0),
        "accepted": draw_accepted(jax.random.fold_in(splits[9], 71), 0),
        "prompt_kv": draw_prompt_kv(jax.random.fold_in(splits[9], 71), 0),
        "out_weight": gaussian(splits[8], (D, D), HD ** -0.5, 0.5, ((0, 4),)),
    }


def ancestry(parents):
    node_count = parents.shape[1]
    positions = jnp.arange(node_count, dtype=jnp.int32)
    step_up = (parents[:, :, None] == positions[None, None, :]) & (positions[None, :, None] > 0)
    closure = jnp.where(step_up, 1.0, 0.0).astype(jnp.float32) + jnp.eye(node_count, dtype=jnp.float32)[None]
    for repeat in range(max(1, (node_count - 1).bit_length())):
        closure = jnp.minimum(closure + jnp.einsum('rij,rjk->rik', closure, closure, precision=lax.Precision.HIGHEST), 1.0)
    return closure > 0.5


def reference(queries, tree_kv, suffix_kv, suffix_len, group_ids, parents, accepted, prompt_kv, out_weight):
    closure = ancestry(parents)
    grouped = queries.reshape(REQS, TREE, HEADS, HD)
    own_keys = tree_kv.reshape(REQS, TREE, 2 * HD)
    slot_pos = jnp.arange(SUF, dtype=jnp.int32)

    def one_request(items):
        query_block, tree_block, suffix_block, length, group, related = items
        prompt_block = lax.dynamic_index_in_dim(prompt_kv, group, 0, keepdims=False)
        keys_all = jnp.concatenate([tree_block, suffix_block, prompt_block], axis=0).astype(jnp.float32)
        valid = jnp.concatenate([related, jnp.broadcast_to(slot_pos[None, :] < length, (TREE, SUF)),
                                 jnp.ones((TREE, PROMPT), dtype=bool)], axis=1)
        scores = jnp.einsum('thd,nd->thn', query_block.astype(jnp.float32), keys_all[:, :HD]) * (HD ** -0.5)
        scores = jnp.where(valid[:, None, :], scores, -jnp.inf)
        row_max = jnp.max(scores, axis=-1, keepdims=True)
        weights = jnp.where(valid[:, None, :], jnp.exp(scores - row_max), 0.0)
        rounded = lax.optimization_barrier(weights.astype(jnp.bfloat16)).astype(jnp.float32)
        summed = jnp.einsum('thn,nd->thd', rounded, keys_all[:, HD:])
        return (summed / jnp.sum(weights, axis=-1)[..., None]).astype(jnp.bfloat16)

    attended = lax.map(one_request, (grouped, own_keys, suffix_kv, suffix_len, group_ids, closure))
    layer_output = jnp.dot(attended.reshape(TOKENS, D), out_weight, preferred_element_type=jnp.float32).astype(jnp.bfloat16)
    path_cache = jnp.take_along_axis(own_keys, accepted[:, :, None], axis=1)
    return layer_output, path_cache
```

```python
import functools
import math

import jax
import jax.numpy as jnp
from jax import lax
from jax.experimental import pallas as pl
from jax.experimental.pallas import tpu as pltpu
from jax.sharding import PartitionSpec as P

neg_large = -1e30
vmem_bytes = 40 * 1024 * 1024


def split_gather(shard, req_count, tp_count):
    if req_count != 8 or tp_count % 2:
        return [lax.all_gather(shard, "req", axis=1, tiled=True)[None]]
    masks = ((7, 6, 1), (5, 4, 3, 2))
    arrived = []
    for step in range(4):
        pairs = []
        for r in range(req_count):
            for t in range(tp_count):
                mine = masks[t % 2]
                if step < len(mine):
                    pairs.append((r * tp_count + t, (r ^ mine[step]) * tp_count + t))
        arrived.append(lax.ppermute(shard, ("req", "tp"), pairs))
    swapped = [swap_in_pair(piece, tp_count) for piece in arrived]
    last = arrived[3] + swapped[3]
    return [shard[None], *(piece[None] for piece in arrived[:3]), *(piece[None] for piece in swapped[:3]), last[None]]


def swap_in_pair(array, tp_count):
    return lax.ppermute(array, "tp", [(t, t ^ 1) for t in range(tp_count)])


def trees_kernel(parents_ref, accepted_ref, tree_ref, bias_ref, path_ref):
    requests, node_count = parents_ref.shape
    path_length = accepted_ref.shape[1]
    above = lax.broadcasted_iota(jnp.int32, (node_count, node_count), 0)
    below = lax.broadcasted_iota(jnp.int32, (node_count, node_count), 1)
    node = lax.broadcasted_iota(jnp.int32, (node_count, path_length), 0)
    closures = []
    for r in range(requests):
        parent = jnp.broadcast_to(parents_ref[r : r + 1, :], (node_count, node_count))
        step = ((parent == above) & (below > 0)) | (above == below)
        closures.append(jnp.where(step, 1.0, 0.0).astype(jnp.bfloat16))
    for repeat in range(max(1, (node_count - 1).bit_length())):
        closures = [jnp.dot(c, c, preferred_element_type=jnp.float32) for c in closures]
        closures = [jnp.where(c > 0.5, 1.0, 0.0).astype(jnp.bfloat16) for c in closures]
    for r in range(requests):
        related = closures[r].astype(jnp.float32).T
        rows = slice(r * node_count, (r + 1) * node_count)
        bias_ref[rows, :] = jnp.where(related > 0.5, 0.0, neg_large)
        chosen = jnp.broadcast_to(accepted_ref[r : r + 1, :], (node_count, path_length)) == node
        path_ref[r] = lax.dot_general(
            jnp.where(chosen, 1.0, 0.0).astype(jnp.bfloat16),
            tree_ref[rows, :],
            (((0,), (0,)), ((), ())),
            preferred_element_type=jnp.float32,
        ).astype(jnp.bfloat16)


def trees(parents, accepted, tree_kv):
    requests, node_count = parents.shape
    return pl.pallas_call(
        trees_kernel,
        out_shape=(
            jax.ShapeDtypeStruct((requests * node_count, node_count), jnp.float32),
            jax.ShapeDtypeStruct((requests, accepted.shape[1], tree_kv.shape[1]), jnp.bfloat16),
        ),
        name="trees",
        cost_estimate=pl.CostEstimate(flops=4_000_000_000, bytes_accessed=400_000, transcendentals=0),
    )(parents, accepted, tree_kv)


def chunk_kernel(unit, piece_count, place_ref, length_ref, group_ref, own_ref, other_ref, bias_ref, tree_ref, suffix_ref, *rest):
    pieces, (weight_own_ref, weight_other_ref, out_ref, attended_ref) = rest[:piece_count], rest[piece_count:]
    node_count = bias_ref.shape[1]
    head_size = tree_ref.shape[1] // 2
    heads = own_ref.shape[1] // head_size
    slot_count = suffix_ref.shape[1]
    rate = head_size**-0.5 * math.log2(math.e)
    slot = lax.broadcasted_iota(jnp.int32, (1, slot_count), 1)

    def against(query, keys):
        return lax.dot_general(query, keys, (((1,), (1,)), ((), ())), preferred_element_type=jnp.float32)

    def summed(weights, values):
        return jnp.dot(weights.astype(jnp.bfloat16), values, preferred_element_type=jnp.float32)

    for number in range(out_ref.shape[0] // unit):
        row = pl.multiple_of(place_ref[0] + number * unit, unit)
        request = row // node_count
        query = jnp.concatenate(
            [ref[pl.ds(row, unit), h * head_size : (h + 1) * head_size] for ref in (own_ref, other_ref) for h in range(heads)], axis=0
        )
        tree = tree_ref[pl.ds(pl.multiple_of(request * node_count, node_count), node_count), :]
        suffix = suffix_ref[request]
        group = group_ref[request]
        prompts = [ref[k, group] for ref in pieces for k in range(ref.shape[0])]
        bias = jnp.concatenate([bias_ref[pl.ds(row, unit), :]] * (2 * heads), axis=0)
        blocks = [(against(query, tree[:, :head_size]) + bias, tree[:, head_size:])]
        used = jnp.where(slot < length_ref[request], 0.0, neg_large)
        blocks.append((against(query, suffix[:, :head_size]) + used, suffix[:, head_size:]))
        prompt = prompts[0] if len(prompts) == 1 else jnp.concatenate(prompts, axis=0)
        blocks.append((against(query, prompt[:, :head_size]), prompt[:, head_size:]))
        largest = functools.reduce(jnp.maximum, [jnp.max(s, axis=1, keepdims=True) for s, _ in blocks])
        total, result = 0.0, 0.0
        for score, values in blocks:
            weight = jnp.exp2((score - largest) * rate)
            total = total + jnp.sum(weight, axis=1, keepdims=True)
            result = result + summed(weight, values)
        attended = (result / total).astype(jnp.bfloat16)
        for h in range(2 * heads):
            attended_ref[number * unit : (number + 1) * unit, h * head_size : (h + 1) * head_size] = attended[h * unit : (h + 1) * unit]
    width = heads * head_size
    columns = 512 if out_ref.shape[1] % 512 == 0 else out_ref.shape[1]
    for c in range(0, out_ref.shape[1], columns):
        product = jnp.dot(attended_ref[:, :width], weight_own_ref[:, c : c + columns], preferred_element_type=jnp.float32) + jnp.dot(
            attended_ref[:, width:], weight_other_ref[:, c : c + columns], preferred_element_type=jnp.float32
        )
        out_ref[:, c : c + columns] = product.astype(out_ref.dtype)


def chunk(place, dtype, chunk_rows, lengths, groups, own, other, bias, tree_kv, suffix_kv, pieces, weight_own, weight_other, name):
    unit = math.gcd(chunk_rows, bias.shape[1])
    in_smem = pl.BlockSpec(memory_space=pltpu.SMEM)
    in_vmem = pl.BlockSpec(memory_space=pltpu.VMEM)
    return pl.pallas_call(
        functools.partial(chunk_kernel, unit, len(pieces)),
        in_specs=[in_smem] * 3 + [in_vmem] * (7 + len(pieces)),
        out_specs=in_vmem,
        out_shape=jax.ShapeDtypeStruct((chunk_rows, weight_own.shape[1]), dtype),
        scratch_shapes=[pltpu.VMEM((chunk_rows, 2 * own.shape[1]), jnp.bfloat16)],
        compiler_params=pltpu.CompilerParams(vmem_limit_bytes=vmem_bytes),
        name=name,
        cost_estimate=pl.CostEstimate(flops=4_000_000_000, bytes_accessed=6_000_000, transcendentals=0),
    )(place, lengths, groups, own, other, bias, tree_kv, suffix_kv, *pieces, weight_own, weight_other)


def local(req_count, tp_count, queries, tree_kv, suffix_kv, suffix_len, group_ids, parents, accepted, prompt_kv, out_weight):
    pieces = split_gather(prompt_kv, req_count, tp_count)
    other_queries = swap_in_pair(queries, tp_count)
    other_weight = swap_in_pair(out_weight, tp_count)
    bias, path_cache = trees(parents, accepted, tree_kv)
    chunk_rows = queries.shape[0] // tp_count
    me = lax.axis_index("tp")
    places = [jnp.reshape(t * chunk_rows, (1,)).astype(jnp.int32) for t in (me ^ 2, me)]
    common = (suffix_len, group_ids, queries, other_queries, bias, tree_kv, suffix_kv, pieces, out_weight, other_weight)
    far = chunk(places[0], jnp.bfloat16, chunk_rows, *common, "far_chunk")
    arrived = lax.ppermute(far, "tp", [(t, t ^ 2) for t in range(tp_count)])
    near = chunk(places[1], jnp.float32, chunk_rows, *common, "near_chunk")
    layer_output = (near + arrived.astype(jnp.float32)).astype(jnp.bfloat16)
    return (layer_output, path_cache)


def solution(mesh):
    return jax.shard_map(
        functools.partial(local, mesh.shape["req"], mesh.shape["tp"]),
        mesh=mesh,
        in_specs=(
            P("req", "tp"),
            P("req", None),
            P("req", None, None),
            P("req"),
            P("req"),
            P("req", None),
            P("req", None),
            P(None, "req", None),
            P("tp", None),
        ),
        out_specs=(P(("req", "tp"), None), P("req", None, None)),
        check_vma=False,
    )
```

```python
import functools
import math

import jax
import jax.numpy as jnp
from jax import lax
from jax.experimental import pallas as pl
from jax.experimental.pallas import tpu as pltpu
from jax.sharding import PartitionSpec as P

neg_large = -1e30
vmem_bytes = 12 * 1024 * 1024


def fetch_shards(shard, req_count, tp_count):
    masks = ((7, 6, 1), (5, 4, 3, 2))
    arrived = []
    for step in range(4):
        pairs = []
        for r in range(req_count):
            for t in range(tp_count):
                mine = masks[t % 2]
                if step < len(mine):
                    pairs.append((r * tp_count + t, (r ^ mine[step]) * tp_count + t))
        arrived.append(lax.ppermute(shard, ("req", "tp"), pairs))
    return arrived


def after(array, earlier):
    return lax.optimization_barrier((array, earlier))[0]


def swap_in_pair(array, tp_count):
    return lax.ppermute(array, "tp", [(t, t ^ 1) for t in range(tp_count)])


def score(query, keys):
    return lax.dot_general(query, keys, (((1,), (1,)), ((), ())), preferred_element_type=jnp.float32)


def stacked_heads(ref, row, unit, head_size):
    return jnp.concatenate([ref[pl.ds(row, unit), h : h + head_size] for h in range(0, ref.shape[1], head_size)], axis=0)


def log2_rate(head_size):
    return head_size**-0.5 * math.log2(math.e)


def absorb(blocks, rate):
    largest = functools.reduce(jnp.maximum, [jnp.max(s, axis=1, keepdims=True) for s, _ in blocks])
    total, result = 0.0, 0.0
    for scores, values in blocks:
        weight = jnp.exp2((scores - largest) * rate)
        total = total + jnp.sum(weight, axis=1, keepdims=True)
        result = result + jnp.dot(weight.astype(jnp.bfloat16), values, preferred_element_type=jnp.float32)
    return largest, total, result


def private_blocks(query, row, unit, length, bias_ref, tree_ref, suffix):
    node_count = bias_ref.shape[1]
    head_size = tree_ref.shape[1] // 2
    request = row // node_count
    tree = tree_ref[pl.ds(pl.multiple_of(request * node_count, node_count), node_count), :]
    bias = jnp.concatenate([bias_ref[pl.ds(row, unit), :]] * (query.shape[0] // unit), axis=0)
    slot = lax.broadcasted_iota(jnp.int32, (1, suffix.shape[0]), 1)
    used = jnp.where(slot < length, 0.0, neg_large)
    return [
        (score(query, tree[:, :head_size]) + bias, tree[:, head_size:]),
        (score(query, suffix[:, :head_size]) + used, suffix[:, head_size:]),
    ]


def prompt_of(pieces, group):
    if len(pieces) == 1:
        return pieces[0][group]
    return jnp.concatenate([ref[group] for ref in pieces[:4]] + [ref[group] for ref in pieces[5:8]] + [pieces[4][group] + pieces[8][group]], axis=0)


def project(attended_ref, weight_own_ref, weight_other_ref, out_ref):
    width = weight_own_ref.shape[0]
    columns = 512 if out_ref.shape[1] % 512 == 0 else out_ref.shape[1]
    for c in range(0, out_ref.shape[1], columns):
        product = jnp.dot(attended_ref[:, :width], weight_own_ref[:, c : c + columns], preferred_element_type=jnp.float32)
        product += jnp.dot(attended_ref[:, width:], weight_other_ref[:, c : c + columns], preferred_element_type=jnp.float32)
        out_ref[:, c : c + columns] = product.astype(out_ref.dtype)


def put_heads(attended_ref, number, unit, attended):
    head_size = attended.shape[1]
    for h in range(attended.shape[0] // unit):
        attended_ref[number * unit : (number + 1) * unit, h * head_size : (h + 1) * head_size] = attended[h * unit : (h + 1) * unit]


def first_row(chunk_rows, offset):
    return (lax.axis_index("tp") ^ offset) * chunk_rows


def prepare_kernel(
    unit, chunk_rows, parents_hbm, accepted_hbm, length_hbm, group_hbm, own_hbm, tree_hbm, suffix_hbm, shard_hbm, weight_hbm, other_ref,
    bias_ref, path_ref, state_ref, own_ref, shard_ref, weight_ref, parents_ref, accepted_ref, length_ref, group_ref, tree_ref, suffix_ref, arrival
):
    requests, node_count = parents_ref.shape
    path_length = accepted_ref.shape[1]
    head_size = tree_ref.shape[1] // 2
    start = pl.multiple_of(first_row(chunk_rows, 2), unit)
    base = jnp.minimum(start // node_count, requests - suffix_ref.shape[0])
    copies = [
        pltpu.make_async_copy(source, target, arrival.at[place])
        for place, (source, target) in enumerate((
            (parents_hbm, parents_ref),
            (accepted_hbm, accepted_ref),
            (tree_hbm, tree_ref),
            (length_hbm, length_ref),
            (group_hbm, group_ref),
            (own_hbm.at[pl.ds(start, chunk_rows)], own_ref),
            (suffix_hbm.at[pl.ds(base, suffix_ref.shape[0])], suffix_ref),
            (shard_hbm, shard_ref),
            (weight_hbm, weight_ref),
        ))
    ]
    for copy in copies:
        copy.start()
    for copy in copies[:3]:
        copy.wait()
    above = lax.broadcasted_iota(jnp.int32, (node_count, node_count), 0)
    below = lax.broadcasted_iota(jnp.int32, (node_count, node_count), 1)
    node = lax.broadcasted_iota(jnp.int32, (node_count, path_length), 0)
    closures = []
    for r in range(requests):
        parent = jnp.broadcast_to(parents_ref[r : r + 1, :], (node_count, node_count))
        step = ((parent == above) & (below > 0)) | (above == below)
        closures.append(jnp.where(step, 1.0, 0.0).astype(jnp.bfloat16))
    for repeat in range(max(1, (node_count - 1).bit_length())):
        closures = [jnp.dot(c, c, preferred_element_type=jnp.float32) for c in closures]
        closures = [jnp.where(c > 0.5, 1.0, 0.0).astype(jnp.bfloat16) for c in closures]
    for r in range(requests):
        related = closures[r].astype(jnp.float32).T
        rows = slice(r * node_count, (r + 1) * node_count)
        bias_ref[rows, :] = jnp.where(related > 0.5, 0.0, neg_large)
        chosen = jnp.broadcast_to(accepted_ref[r : r + 1, :], (node_count, path_length)) == node
        path_ref[r] = lax.dot_general(
            jnp.where(chosen, 1.0, 0.0).astype(jnp.bfloat16),
            tree_ref[rows, :],
            (((0,), (0,)), ((), ())),
            preferred_element_type=jnp.float32,
        ).astype(jnp.bfloat16)
    for copy in copies[3:7]:
        copy.wait()
    for number in range(chunk_rows // unit):
        row = pl.multiple_of(start + number * unit, unit)
        request = row // node_count
        query = jnp.concatenate(
            [stacked_heads(own_ref, number * unit, unit, head_size), stacked_heads(other_ref, row, unit, head_size)], axis=0
        )
        blocks = private_blocks(query, row, unit, length_ref[request], bias_ref, tree_ref, suffix_ref[request - base])
        largest, total, result = absorb(blocks, log2_rate(head_size))
        lanes = result.shape
        rows = slice(number * lanes[0], (number + 1) * lanes[0])
        group = group_ref[request].astype(jnp.float32)
        for place, value in enumerate((result, largest, total, group)):
            state_ref[rows, place * head_size : (place + 1) * head_size] = jnp.broadcast_to(value, lanes)
    for copy in copies[7:]:
        copy.wait()


def in_smem():
    return pl.BlockSpec(memory_space=pltpu.SMEM)


def in_vmem():
    return pl.BlockSpec(memory_space=pltpu.VMEM)


def prepare(unit, chunk_rows, parents, accepted, lengths, groups, own, tree_kv, suffix_kv, shard, weight, other):
    requests, node_count = parents.shape
    head_size = tree_kv.shape[1] // 2
    state_rows = chunk_rows * 2 * (own.shape[1] // head_size)
    touched = min(requests, -(-(chunk_rows + node_count - unit) // node_count))
    sources = [pltpu.with_memory_space_constraint(a, pltpu.HBM) for a in (parents, accepted, lengths, groups, own, tree_kv, suffix_kv, shard, weight)]
    return pl.pallas_call(
        functools.partial(prepare_kernel, unit, chunk_rows),
        in_specs=[pl.BlockSpec(memory_space=pltpu.HBM)] * 9 + [in_vmem()],
        out_specs=[in_vmem()] * 6,
        out_shape=(
            jax.ShapeDtypeStruct((requests * node_count, node_count), jnp.float32),
            jax.ShapeDtypeStruct((requests, accepted.shape[1], tree_kv.shape[1]), jnp.bfloat16),
            jax.ShapeDtypeStruct((state_rows, 4 * head_size), jnp.float32),
            jax.ShapeDtypeStruct((chunk_rows, own.shape[1]), own.dtype),
            jax.ShapeDtypeStruct(shard.shape, shard.dtype),
            jax.ShapeDtypeStruct(weight.shape, weight.dtype),
        ),
        scratch_shapes=[
            pltpu.VMEM(parents.shape, jnp.int32),
            pltpu.VMEM(accepted.shape, jnp.int32),
            pltpu.SMEM(lengths.shape, jnp.int32),
            pltpu.SMEM(groups.shape, jnp.int32),
            pltpu.VMEM(tree_kv.shape, tree_kv.dtype),
            pltpu.VMEM((touched, *suffix_kv.shape[1:]), suffix_kv.dtype),
            pltpu.SemaphoreType.DMA((9,)),
        ],
        compiler_params=pltpu.CompilerParams(vmem_limit_bytes=vmem_bytes),
        name="prepare",
        cost_estimate=pl.CostEstimate(flops=400_000_000, bytes_accessed=2_000_000, transcendentals=0),
    )(*sources, other)


def far_kernel(unit, piece_count, own_ref, other_ref, state_ref, *rest):
    pieces, (weight_own_ref, weight_other_ref, out_ref, attended_ref) = rest[:piece_count], rest[piece_count:]
    chunk_rows = out_ref.shape[0]
    head_size = state_ref.shape[1] // 4
    rate = log2_rate(head_size)
    group_count = pieces[0].shape[0]
    prompts = [prompt_of(pieces, g) for g in range(group_count)]
    start = first_row(chunk_rows, 2)
    for number in range(chunk_rows // unit):
        row = pl.multiple_of(start + number * unit, unit)
        query = jnp.concatenate(
            [stacked_heads(own_ref, number * unit, unit, head_size), stacked_heads(other_ref, row, unit, head_size)], axis=0
        )
        rows = slice(number * query.shape[0], (number + 1) * query.shape[0])
        before, largest, total, group = (state_ref[rows, place * head_size : (place + 1) * head_size] for place in range(4))
        prompt = prompts[0]
        for g in range(1, group_count):
            mine = jnp.broadcast_to(group[:1, :1], prompt.shape) == g
            prompt = jnp.where(mine, prompts[g], prompt)
        scores = score(query, prompt[:, :head_size])
        top = jnp.maximum(largest[:, :1], jnp.max(scores, axis=1, keepdims=True))
        weight = jnp.exp2((scores - top) * rate)
        fade = jnp.exp2((largest[:, :1] - top) * rate)
        total = total[:, :1] * fade + jnp.sum(weight, axis=1, keepdims=True)
        result = before * fade + jnp.dot(weight.astype(jnp.bfloat16), prompt[:, head_size:], preferred_element_type=jnp.float32)
        put_heads(attended_ref, number, unit, (result / total).astype(jnp.bfloat16))
    project(attended_ref, weight_own_ref, weight_other_ref, out_ref)


def near_kernel(unit, piece_count, length_ref, group_ref, own_ref, other_ref, bias_ref, tree_ref, suffix_ref, *rest):
    pieces, (weight_own_ref, weight_other_ref, out_ref, attended_ref) = rest[:piece_count], rest[piece_count:]
    chunk_rows = out_ref.shape[0]
    head_size = tree_ref.shape[1] // 2
    start = first_row(chunk_rows, 0)
    for number in range(chunk_rows // unit):
        row = pl.multiple_of(start + number * unit, unit)
        query = jnp.concatenate([stacked_heads(ref, row, unit, head_size) for ref in (own_ref, other_ref)], axis=0)
        request = row // bias_ref.shape[1]
        blocks = private_blocks(query, row, unit, length_ref[request], bias_ref, tree_ref, suffix_ref[request])
        prompt = prompt_of(pieces, group_ref[request])
        blocks.append((score(query, prompt[:, :head_size]), prompt[:, head_size:]))
        largest, total, result = absorb(blocks, log2_rate(head_size))
        put_heads(attended_ref, number, unit, (result / total).astype(jnp.bfloat16))
    project(attended_ref, weight_own_ref, weight_other_ref, out_ref)


def chunk(kernel, name, dtype, scalars, arrays, chunk_rows, weights):
    in_specs = [in_smem()] * len(scalars) + [in_vmem()] * (len(arrays) + len(weights))
    return pl.pallas_call(
        kernel,
        in_specs=in_specs,
        out_specs=in_vmem(),
        out_shape=jax.ShapeDtypeStruct((chunk_rows, weights[0].shape[1]), dtype),
        scratch_shapes=[pltpu.VMEM((chunk_rows, 2 * weights[0].shape[0]), jnp.bfloat16)],
        compiler_params=pltpu.CompilerParams(vmem_limit_bytes=vmem_bytes),
        name=name,
        cost_estimate=pl.CostEstimate(flops=500_000_000, bytes_accessed=1_000_000, transcendentals=0),
    )(*scalars, *arrays, *weights)


def local(req_count, tp_count, queries, tree_kv, suffix_kv, suffix_len, group_ids, parents, accepted, prompt_kv, out_weight):
    chunk_rows = queries.shape[0] // tp_count
    unit = math.gcd(chunk_rows, parents.shape[1])
    other_queries = swap_in_pair(queries, tp_count)
    if req_count == 8 and tp_count % 2 == 0:
        fetched = fetch_shards(prompt_kv, req_count, tp_count)
        other_weight = swap_in_pair(out_weight, tp_count)
    else:
        fetched = None
        other_weight = swap_in_pair(out_weight, tp_count)
    bias, path_cache, state, far_queries, shard, own_weight = prepare(
        unit, chunk_rows, parents, accepted, suffix_len, group_ids, queries, tree_kv, suffix_kv, prompt_kv, out_weight, other_queries
    )
    if fetched is None:
        pieces = [lax.all_gather(prompt_kv, "req", axis=1, tiled=True)]
    else:
        pieces = [shard, *fetched, *(swap_in_pair(after(piece, state), tp_count) for piece in fetched)]
    weights = (own_weight, other_weight)
    far = chunk(
        functools.partial(far_kernel, unit, len(pieces)), "far_chunk", jnp.bfloat16, (), (far_queries, other_queries, state, *pieces), chunk_rows, weights
    )
    arrived = lax.ppermute(far, "tp", [(t, t ^ 2) for t in range(tp_count)])
    near = chunk(
        functools.partial(near_kernel, unit, len(pieces)), "near_chunk", jnp.float32, (suffix_len, group_ids),
        (queries, other_queries, bias, tree_kv, suffix_kv, *pieces), chunk_rows, weights
    )
    layer_output = (near + arrived.astype(jnp.float32)).astype(jnp.bfloat16)
    return (layer_output, path_cache)


def solution(mesh):
    return jax.shard_map(
        functools.partial(local, mesh.shape["req"], mesh.shape["tp"]),
        mesh=mesh,
        in_specs=(
            P("req", "tp"),
            P("req", None),
            P("req", None, None),
            P("req"),
            P("req"),
            P("req", None),
            P("req", None),
            P(None, "req", None),
            P("tp", None),
        ),
        out_specs=(P(("req", "tp"), None), P("req", None, None)),
        check_vma=False,
    )
```

```python
import functools
import math

import jax
import jax.numpy as jnp
from jax import lax
from jax.experimental import pallas as pl
from jax.experimental.pallas import tpu as pltpu
from jax.sharding import PartitionSpec as P

neg_large = -1e30
vmem_bytes = 12 * 1024 * 1024


def fetch_shards(shard, req_count, tp_count):
    masks = ((7, 6, 1), (5, 4, 3, 2))
    arrived = []
    for step in range(4):
        pairs = []
        for r in range(req_count):
            for t in range(tp_count):
                mine = masks[t % 2]
                if step < len(mine):
                    pairs.append((r * tp_count + t, (r ^ mine[step]) * tp_count + t))
        arrived.append(lax.ppermute(shard, ("req", "tp"), pairs))
    return arrived


def after(array, earlier):
    return lax.optimization_barrier((array, earlier))[0]


def swap_in_pair(array, tp_count):
    return lax.ppermute(array, "tp", [(t, t ^ 1) for t in range(tp_count)])


def score(query, keys):
    return lax.dot_general(query, keys, (((1,), (1,)), ((), ())), preferred_element_type=jnp.float32)


def stacked_heads(ref, row, unit, head_size):
    return jnp.concatenate([ref[pl.ds(row, unit), h : h + head_size] for h in range(0, ref.shape[1], head_size)], axis=0)


def log2_rate(head_size):
    return head_size**-0.5 * math.log2(math.e)


def absorb(blocks, rate):
    largest = functools.reduce(jnp.maximum, [jnp.max(s, axis=1, keepdims=True) for s, _ in blocks])
    total, result = 0.0, 0.0
    for scores, values in blocks:
        weight = jnp.exp2((scores - largest) * rate)
        total = total + jnp.sum(weight, axis=1, keepdims=True)
        result = result + jnp.dot(weight.astype(jnp.bfloat16), values, preferred_element_type=jnp.float32)
    return largest, total, result


def private_blocks(query, bias, used, tree, suffix):
    head_size = query.shape[1]
    every = jnp.concatenate([bias] * (query.shape[0] // bias.shape[0]), axis=0)
    return [
        (score(query, tree[:, :head_size]) + every, tree[:, head_size:]),
        (score(query, suffix[:, :head_size]) + used, suffix[:, head_size:]),
    ]


def prompt_of(pieces, group):
    if len(pieces) == 1:
        return pieces[0][group]
    shard, fetched, swapped = pieces
    groups = shard.shape[0]
    places = range(group, fetched.shape[0], groups)
    kept = [shard[group]] + [ref[place] for ref in (fetched, swapped) for place in places[:-1]]
    return jnp.concatenate([*kept, fetched[places[-1]] + swapped[places[-1]]], axis=0)


def project(attended_ref, weight_own_ref, weight_other_ref, out_ref):
    width = weight_own_ref.shape[0]
    columns = 512 if out_ref.shape[1] % 512 == 0 else out_ref.shape[1]
    for c in range(0, out_ref.shape[1], columns):
        product = jnp.dot(attended_ref[:, :width], weight_own_ref[:, c : c + columns], preferred_element_type=jnp.float32)
        product += jnp.dot(attended_ref[:, width:], weight_other_ref[:, c : c + columns], preferred_element_type=jnp.float32)
        out_ref[:, c : c + columns] = product.astype(out_ref.dtype)


def put_heads(attended_ref, number, unit, attended):
    head_size = attended.shape[1]
    for h in range(attended.shape[0] // unit):
        attended_ref[number * unit : (number + 1) * unit, h * head_size : (h + 1) * head_size] = attended[h * unit : (h + 1) * unit]


def first_row(chunk_rows, offset):
    return (lax.axis_index("tp") ^ offset) * chunk_rows


def closures(parents, node_count):
    above = lax.broadcasted_iota(jnp.int32, (node_count, node_count), 0)
    below = lax.broadcasted_iota(jnp.int32, (node_count, node_count), 1)
    found = []
    for parent in parents:
        step = ((jnp.broadcast_to(parent, (node_count, node_count)) == above) & (below > 0)) | (above == below)
        found.append(jnp.where(step, 1.0, 0.0).astype(jnp.bfloat16))
    for repeat in range(max(1, (node_count - 1).bit_length())):
        found = [jnp.dot(c, c, preferred_element_type=jnp.float32) for c in found]
        found = [jnp.where(c > 0.5, 1.0, 0.0).astype(jnp.bfloat16) for c in found]
    return found


def bias_of(closure):
    return jnp.where(closure.astype(jnp.float32).T > 0.5, 0.0, neg_large)


def first_request(chunk_rows, offset, node_count, requests, touched):
    return jnp.minimum(first_row(chunk_rows, offset) // node_count, requests - touched)


def load_kernel(
    chunk_rows, parents_hbm, length_hbm, group_hbm, own_hbm, tree_hbm, suffix_hbm, shard_hbm, weight_hbm,
    bias_ref, notes_ref, own_ref, tree_ref, suffix_ref, shard_ref, weight_ref, parents_ref, length_ref, group_ref, arrival
):
    requests, node_count = parents_ref.shape
    touched, slot_count = suffix_ref.shape[:2]
    start = pl.multiple_of(first_row(chunk_rows, 2), math.gcd(chunk_rows, node_count))
    base = first_request(chunk_rows, 2, node_count, requests, touched)
    copies = [
        pltpu.make_async_copy(source, target, arrival.at[place])
        for place, (source, target) in enumerate((
            (parents_hbm, parents_ref),
            (length_hbm, length_ref),
            (group_hbm, group_ref),
            (own_hbm.at[pl.ds(start, chunk_rows)], own_ref),
            (tree_hbm.at[pl.ds(pl.multiple_of(base * node_count, node_count), touched * node_count)], tree_ref),
            (suffix_hbm.at[pl.ds(base, touched)], suffix_ref),
            (shard_hbm, shard_ref),
            (weight_hbm, weight_ref),
        ))
    ]
    for copy in copies:
        copy.start()
    for copy in copies[:3]:
        copy.wait()
    found = closures([parents_ref[pl.ds(base + k, 1), :] for k in range(touched)], node_count)
    slot = lax.broadcasted_iota(jnp.int32, (1, slot_count), 1)
    for k in range(touched):
        bias_ref[k * node_count : (k + 1) * node_count, :] = bias_of(found[k])
        notes_ref[k, :1, :] = jnp.where(slot < length_ref[base + k], 0.0, neg_large)
        notes_ref[k, 1:2, :] = jnp.broadcast_to(group_ref[base + k].astype(jnp.float32), (1, slot_count))
    for copy in copies[3:]:
        copy.wait()


def private_kernel(unit, chunk_rows, node_count, requests, bias_ref, notes_ref, own_ref, tree_ref, suffix_ref, other_ref, state_ref):
    head_size = tree_ref.shape[1] // 2
    touched = suffix_ref.shape[0]
    start = pl.multiple_of(first_row(chunk_rows, 2), unit)
    base = first_request(chunk_rows, 2, node_count, requests, touched)
    for number in range(chunk_rows // unit):
        row = pl.multiple_of(start + number * unit, unit)
        place = row // node_count - base
        query = jnp.concatenate(
            [stacked_heads(own_ref, number * unit, unit, head_size), stacked_heads(other_ref, row, unit, head_size)], axis=0
        )
        bias = bias_ref[pl.ds(pl.multiple_of(row - base * node_count, unit), unit), :]
        tree = tree_ref[pl.ds(pl.multiple_of(place * node_count, node_count), node_count), :]
        blocks = private_blocks(query, bias, notes_ref[place, :1, :], tree, suffix_ref[place])
        largest, total, result = absorb(blocks, log2_rate(head_size))
        lanes = result.shape
        rows = slice(number * lanes[0], (number + 1) * lanes[0])
        for spot, value in enumerate((result, largest, total, notes_ref[place, 1:2, :head_size])):
            state_ref[rows, spot * head_size : (spot + 1) * head_size] = jnp.broadcast_to(value, lanes)


def in_smem():
    return pl.BlockSpec(memory_space=pltpu.SMEM)


def in_vmem():
    return pl.BlockSpec(memory_space=pltpu.VMEM)


def load(unit, chunk_rows, parents, lengths, groups, own, tree_kv, suffix_kv, shard, weight):
    requests, node_count = parents.shape
    touched = min(requests, -(-(chunk_rows + node_count - unit) // node_count))
    sources = [pltpu.with_memory_space_constraint(a, pltpu.HBM) for a in (parents, lengths, groups, own, tree_kv, suffix_kv, shard, weight)]
    return pl.pallas_call(
        functools.partial(load_kernel, chunk_rows),
        in_specs=[pl.BlockSpec(memory_space=pltpu.HBM)] * 8,
        out_specs=[in_vmem()] * 7,
        out_shape=(
            jax.ShapeDtypeStruct((touched * node_count, node_count), jnp.float32),
            jax.ShapeDtypeStruct((touched, 8, suffix_kv.shape[1]), jnp.float32),
            jax.ShapeDtypeStruct((chunk_rows, own.shape[1]), own.dtype),
            jax.ShapeDtypeStruct((touched * node_count, tree_kv.shape[1]), tree_kv.dtype),
            jax.ShapeDtypeStruct((touched, *suffix_kv.shape[1:]), suffix_kv.dtype),
            jax.ShapeDtypeStruct(shard.shape, shard.dtype),
            jax.ShapeDtypeStruct(weight.shape, weight.dtype),
        ),
        scratch_shapes=[
            pltpu.VMEM(parents.shape, jnp.int32),
            pltpu.SMEM(lengths.shape, jnp.int32),
            pltpu.SMEM(groups.shape, jnp.int32),
            pltpu.SemaphoreType.DMA((8,)),
        ],
        compiler_params=pltpu.CompilerParams(vmem_limit_bytes=vmem_bytes),
        name="load",
        cost_estimate=pl.CostEstimate(flops=100_000_000, bytes_accessed=2_000_000, transcendentals=0),
    )(*sources)


def private(unit, chunk_rows, node_count, requests, loaded, other):
    bias, notes, own, tree, suffix = loaded
    head_size = tree.shape[1] // 2
    state_rows = chunk_rows * 2 * (own.shape[1] // head_size)
    return pl.pallas_call(
        functools.partial(private_kernel, unit, chunk_rows, node_count, requests),
        in_specs=[in_vmem()] * 6,
        out_specs=in_vmem(),
        out_shape=jax.ShapeDtypeStruct((state_rows, 4 * head_size), jnp.float32),
        compiler_params=pltpu.CompilerParams(vmem_limit_bytes=vmem_bytes),
        name="private",
        cost_estimate=pl.CostEstimate(flops=300_000_000, bytes_accessed=500_000, transcendentals=0),
    )(*loaded, other)


def far_kernel(unit, piece_count, own_ref, other_ref, state_ref, *rest):
    pieces, (weight_own_ref, weight_other_ref, out_ref, attended_ref) = rest[:piece_count], rest[piece_count:]
    chunk_rows = out_ref.shape[0]
    head_size = state_ref.shape[1] // 4
    rate = log2_rate(head_size)
    group_count = pieces[0].shape[0]
    prompts = [prompt_of(pieces, g) for g in range(group_count)]
    start = first_row(chunk_rows, 2)
    for number in range(chunk_rows // unit):
        row = pl.multiple_of(start + number * unit, unit)
        query = jnp.concatenate(
            [stacked_heads(own_ref, number * unit, unit, head_size), stacked_heads(other_ref, row, unit, head_size)], axis=0
        )
        rows = slice(number * query.shape[0], (number + 1) * query.shape[0])
        before, largest, total, group = (state_ref[rows, place * head_size : (place + 1) * head_size] for place in range(4))
        prompt = prompts[0]
        for g in range(1, group_count):
            mine = jnp.broadcast_to(group[:1, :1], prompt.shape) == g
            prompt = jnp.where(mine, prompts[g], prompt)
        scores = score(query, prompt[:, :head_size])
        top = jnp.maximum(largest[:, :1], jnp.max(scores, axis=1, keepdims=True))
        weight = jnp.exp2((scores - top) * rate)
        fade = jnp.exp2((largest[:, :1] - top) * rate)
        total = total[:, :1] * fade + jnp.sum(weight, axis=1, keepdims=True)
        result = before * fade + jnp.dot(weight.astype(jnp.bfloat16), prompt[:, head_size:], preferred_element_type=jnp.float32)
        put_heads(attended_ref, number, unit, (result / total).astype(jnp.bfloat16))
    project(attended_ref, weight_own_ref, weight_other_ref, out_ref)


def near_kernel(
    unit, piece_count, length_ref, group_ref, own_ref, other_ref, parents_ref, accepted_ref, tree_ref, suffix_ref, *rest
):
    pieces, (weight_own_ref, weight_other_ref, out_ref, path_ref, attended_ref, bias_ref) = rest[:piece_count], rest[piece_count:]
    chunk_rows = out_ref.shape[0]
    requests, node_count = parents_ref.shape
    path_length = accepted_ref.shape[1]
    head_size = tree_ref.shape[1] // 2
    node = lax.broadcasted_iota(jnp.int32, (node_count, path_length), 0)
    for r, closure in enumerate(closures([parents_ref[r : r + 1, :] for r in range(requests)], node_count)):
        rows = slice(r * node_count, (r + 1) * node_count)
        bias_ref[rows, :] = bias_of(closure)
        chosen = jnp.broadcast_to(accepted_ref[r : r + 1, :], (node_count, path_length)) == node
        path_ref[r] = lax.dot_general(
            jnp.where(chosen, 1.0, 0.0).astype(jnp.bfloat16),
            tree_ref[rows, :],
            (((0,), (0,)), ((), ())),
            preferred_element_type=jnp.float32,
        ).astype(jnp.bfloat16)
    prompts = [prompt_of(pieces, g) for g in range(pieces[0].shape[0])]
    slot = lax.broadcasted_iota(jnp.int32, (1, suffix_ref.shape[1]), 1)
    start = first_row(chunk_rows, 0)
    for number in range(chunk_rows // unit):
        row = pl.multiple_of(start + number * unit, unit)
        query = jnp.concatenate([stacked_heads(ref, row, unit, head_size) for ref in (own_ref, other_ref)], axis=0)
        request = row // node_count
        used = jnp.where(slot < length_ref[request], 0.0, neg_large)
        tree = tree_ref[pl.ds(pl.multiple_of(request * node_count, node_count), node_count), :]
        blocks = private_blocks(query, bias_ref[pl.ds(row, unit), :], used, tree, suffix_ref[request])
        group = group_ref[request]
        prompt = functools.reduce(lambda held, g: jnp.where(group == g, prompts[g], held), range(1, len(prompts)), prompts[0])
        blocks.append((score(query, prompt[:, :head_size]), prompt[:, head_size:]))
        largest, total, result = absorb(blocks, log2_rate(head_size))
        put_heads(attended_ref, number, unit, (result / total).astype(jnp.bfloat16))
    project(attended_ref, weight_own_ref, weight_other_ref, out_ref)


def chunk(kernel, name, outs, scalars, arrays, weights, scratch):
    return pl.pallas_call(
        kernel,
        in_specs=[in_smem()] * len(scalars) + [in_vmem()] * (len(arrays) + len(weights)),
        out_specs=[in_vmem()] * len(outs),
        out_shape=outs,
        scratch_shapes=[pltpu.VMEM((outs[0].shape[0], 2 * weights[0].shape[0]), jnp.bfloat16), *scratch],
        compiler_params=pltpu.CompilerParams(vmem_limit_bytes=vmem_bytes),
        name=name,
        cost_estimate=pl.CostEstimate(flops=500_000_000, bytes_accessed=1_000_000, transcendentals=0),
    )(*scalars, *arrays, *weights)


def local(req_count, tp_count, queries, tree_kv, suffix_kv, suffix_len, group_ids, parents, accepted, prompt_kv, out_weight):
    chunk_rows = queries.shape[0] // tp_count
    unit = math.gcd(chunk_rows, parents.shape[1])
    other_queries = swap_in_pair(queries, tp_count)
    if req_count == 8 and tp_count % 2 == 0:
        fetched = fetch_shards(prompt_kv, req_count, tp_count)
        other_weight = swap_in_pair(out_weight, tp_count)
    else:
        fetched = None
        other_weight = swap_in_pair(out_weight, tp_count)
    requests, node_count = parents.shape
    *loaded, shard, own_weight = load(unit, chunk_rows, parents, suffix_len, group_ids, queries, tree_kv, suffix_kv, prompt_kv, out_weight)
    state = private(unit, chunk_rows, node_count, requests, loaded, other_queries)
    if fetched is None:
        pieces = [lax.all_gather(prompt_kv, "req", axis=1, tiled=True)]
    else:
        joined = jnp.concatenate([after(piece, shard) for piece in fetched], axis=0)
        pieces = [shard, joined, swap_in_pair(joined, tp_count)]
    weights = (own_weight, other_weight)
    chunk_shape = (chunk_rows, out_weight.shape[1])
    (far,) = chunk(
        functools.partial(far_kernel, unit, len(pieces)), "far_chunk", [jax.ShapeDtypeStruct(chunk_shape, jnp.bfloat16)],
        (), (loaded[2], other_queries, state, *pieces), weights, ()
    )
    arrived = lax.ppermute(far, "tp", [(t, t ^ 2) for t in range(tp_count)])
    near, path_cache = chunk(
        functools.partial(near_kernel, unit, len(pieces)), "near_chunk",
        [jax.ShapeDtypeStruct(chunk_shape, jnp.float32), jax.ShapeDtypeStruct((*accepted.shape, tree_kv.shape[1]), jnp.bfloat16)],
        (suffix_len, group_ids), (queries, other_queries, parents, accepted, tree_kv, suffix_kv, *pieces), weights,
        (pltpu.VMEM((requests * node_count, node_count), jnp.float32),)
    )
    layer_output = (near + arrived.astype(jnp.float32)).astype(jnp.bfloat16)
    return (layer_output, path_cache)


def solution(mesh):
    return jax.shard_map(
        functools.partial(local, mesh.shape["req"], mesh.shape["tp"]),
        mesh=mesh,
        in_specs=(
            P("req", "tp"),
            P("req", None),
            P("req", None, None),
            P("req"),
            P("req"),
            P("req", None),
            P("req", None),
            P(None, "req", None),
            P("tp", None),
        ),
        out_specs=(P(("req", "tp"), None), P("req", None, None)),
        check_vma=False,
    )
```

```python
import functools
import math

import jax
import jax.numpy as jnp
from jax import lax
from jax.experimental import pallas as pl
from jax.experimental.pallas import tpu as pltpu
from jax.sharding import PartitionSpec as P

neg_large = -1e30
vmem_bytes = 12 * 1024 * 1024
fetches = 4


def fetch_shards(shard, req_count, tp_count):
    masks = ((7, 4, 3), (6, 5, 2, 1))
    arrived = []
    for step in range(fetches):
        pairs = []
        for r in range(req_count):
            for t in range(tp_count):
                mine = masks[t % 2]
                if step < len(mine):
                    pairs.append((r * tp_count + t, (r ^ mine[step]) * tp_count + t))
        arrived.append(lax.ppermute(shard, ("req", "tp"), pairs))
    return arrived


def after(array, earlier):
    return lax.optimization_barrier((array, earlier))[0]


def swap_in_pair(array, tp_count):
    return lax.ppermute(array, "tp", [(t, t ^ 1) for t in range(tp_count)])


def score(query, keys):
    return lax.dot_general(query, keys, (((1,), (1,)), ((), ())), preferred_element_type=jnp.float32)


def stacked_heads(ref, row, unit, head_size):
    return jnp.concatenate([ref[pl.ds(row, unit), h : h + head_size] for h in range(0, ref.shape[1], head_size)], axis=0)


def log2_rate(head_size):
    return head_size**-0.5 * math.log2(math.e)


def absorb(blocks, rate):
    largest = functools.reduce(jnp.maximum, [jnp.max(s, axis=1, keepdims=True) for s, _ in blocks])
    total, result = 0.0, 0.0
    for scores, values in blocks:
        weight = jnp.exp2((scores - largest) * rate)
        total = total + jnp.sum(weight, axis=1, keepdims=True)
        result = result + jnp.dot(weight.astype(jnp.bfloat16), values, preferred_element_type=jnp.float32)
    return largest, total, result


def private_blocks(query, bias, used, tree, suffix):
    head_size = query.shape[1]
    every = jnp.concatenate([bias] * (query.shape[0] // bias.shape[0]), axis=0)
    return [
        (score(query, tree[:, :head_size]) + every, tree[:, head_size:]),
        (score(query, suffix[:, :head_size]) + used, suffix[:, head_size:]),
    ]


def prompt_of(prompts, group):
    return functools.reduce(lambda held, g: jnp.where(group == g, prompts[g], held), range(1, len(prompts)), prompts[0])


def kept_prompts(shard, fetched):
    groups = shard.shape[0]
    return [jnp.concatenate([shard[g]] + [fetched[k + g] for k in range(0, fetched.shape[0] - groups, groups)], axis=0) for g in range(groups)]


def swapped_prompts(fetched, swapped, groups):
    last = swapped.shape[0] - groups
    return [jnp.concatenate([swapped[k + g] for k in range(0, last, groups)] + [fetched[last + g] + swapped[last + g]], axis=0) for g in range(groups)]


def project(attended_ref, weight_own_ref, weight_other_ref, out_ref):
    width = weight_own_ref.shape[0]
    columns = 512 if out_ref.shape[1] % 512 == 0 else out_ref.shape[1]
    for c in range(0, out_ref.shape[1], columns):
        product = jnp.dot(attended_ref[:, :width], weight_own_ref[:, c : c + columns], preferred_element_type=jnp.float32)
        product += jnp.dot(attended_ref[:, width:], weight_other_ref[:, c : c + columns], preferred_element_type=jnp.float32)
        out_ref[:, c : c + columns] = product.astype(out_ref.dtype)


def put_heads(attended_ref, number, unit, attended):
    head_size = attended.shape[1]
    for h in range(attended.shape[0] // unit):
        attended_ref[number * unit : (number + 1) * unit, h * head_size : (h + 1) * head_size] = attended[h * unit : (h + 1) * unit]


def first_row(chunk_rows, offset):
    return (lax.axis_index("tp") ^ offset) * chunk_rows


def closures(parents, node_count):
    above = lax.broadcasted_iota(jnp.int32, (node_count, node_count), 0)
    below = lax.broadcasted_iota(jnp.int32, (node_count, node_count), 1)
    found = []
    for parent in parents:
        step = ((jnp.broadcast_to(parent, (node_count, node_count)) == above) & (below > 0)) | (above == below)
        found.append(jnp.where(step, 1.0, 0.0).astype(jnp.bfloat16))
    for repeat in range(max(1, (node_count - 1).bit_length())):
        found = [jnp.dot(c, c, preferred_element_type=jnp.float32) for c in found]
        found = [jnp.where(c > 0.5, 1.0, 0.0).astype(jnp.bfloat16) for c in found]
    return found


def bias_of(closure):
    return jnp.where(closure.astype(jnp.float32).T > 0.5, 0.0, neg_large)


def first_request(chunk_rows, offset, node_count, requests, touched):
    return jnp.minimum(first_row(chunk_rows, offset) // node_count, requests - touched)


def load_kernel(
    chunk_rows, parents_hbm, length_hbm, group_hbm, own_hbm, tree_hbm, suffix_hbm, shard_hbm, weight_hbm,
    bias_ref, notes_ref, own_ref, tree_ref, suffix_ref, shard_ref, weight_ref, parents_ref, length_ref, group_ref, arrival
):
    requests, node_count = parents_ref.shape
    touched, slot_count = suffix_ref.shape[:2]
    start = pl.multiple_of(first_row(chunk_rows, 2), math.gcd(chunk_rows, node_count))
    base = first_request(chunk_rows, 2, node_count, requests, touched)
    copies = [
        pltpu.make_async_copy(source, target, arrival.at[place])
        for place, (source, target) in enumerate((
            (parents_hbm, parents_ref),
            (length_hbm, length_ref),
            (group_hbm, group_ref),
            (own_hbm.at[pl.ds(start, chunk_rows)], own_ref),
            (tree_hbm.at[pl.ds(pl.multiple_of(base * node_count, node_count), touched * node_count)], tree_ref),
            (suffix_hbm.at[pl.ds(base, touched)], suffix_ref),
            (shard_hbm, shard_ref),
            (weight_hbm, weight_ref),
        ))
    ]
    for copy in copies:
        copy.start()
    for copy in copies[:3]:
        copy.wait()
    found = closures([parents_ref[pl.ds(base + k, 1), :] for k in range(touched)], node_count)
    slot = lax.broadcasted_iota(jnp.int32, (1, slot_count), 1)
    for k in range(touched):
        bias_ref[k * node_count : (k + 1) * node_count, :] = bias_of(found[k])
        notes_ref[k, :1, :] = jnp.where(slot < length_ref[base + k], 0.0, neg_large)
        notes_ref[k, 1:2, :] = jnp.broadcast_to(group_ref[base + k].astype(jnp.float32), (1, slot_count))
    for copy in copies[3:]:
        copy.wait()


def private_kernel(unit, chunk_rows, node_count, requests, bias_ref, notes_ref, own_ref, tree_ref, suffix_ref, other_ref, *rest):
    head_size = tree_ref.shape[1] // 2
    touched = suffix_ref.shape[0]
    *parts, state_ref = rest
    prompts = kept_prompts(*parts) if parts else []
    start = pl.multiple_of(first_row(chunk_rows, 2), unit)
    base = first_request(chunk_rows, 2, node_count, requests, touched)
    for number in range(chunk_rows // unit):
        row = pl.multiple_of(start + number * unit, unit)
        place = row // node_count - base
        query = jnp.concatenate(
            [stacked_heads(own_ref, number * unit, unit, head_size), stacked_heads(other_ref, row, unit, head_size)], axis=0
        )
        bias = bias_ref[pl.ds(pl.multiple_of(row - base * node_count, unit), unit), :]
        tree = tree_ref[pl.ds(pl.multiple_of(place * node_count, node_count), node_count), :]
        notes = notes_ref[place]
        group = notes[1:2]
        blocks = private_blocks(query, bias, notes[:1], tree, suffix_ref[place])
        if prompts:
            prompt = prompt_of(prompts, group[:, : 2 * head_size])
            blocks.append((score(query, prompt[:, :head_size]), prompt[:, head_size:]))
        largest, total, result = absorb(blocks, log2_rate(head_size))
        lanes = result.shape
        rows = slice(number * lanes[0], (number + 1) * lanes[0])
        for spot, value in enumerate((result, largest, total, group[:, :head_size])):
            state_ref[rows, spot * head_size : (spot + 1) * head_size] = jnp.broadcast_to(value, lanes)


def in_smem():
    return pl.BlockSpec(memory_space=pltpu.SMEM)


def in_vmem():
    return pl.BlockSpec(memory_space=pltpu.VMEM)


def load(unit, chunk_rows, parents, lengths, groups, own, tree_kv, suffix_kv, shard, weight):
    requests, node_count = parents.shape
    touched = min(requests, -(-(chunk_rows + node_count - unit) // node_count))
    sources = [pltpu.with_memory_space_constraint(a, pltpu.HBM) for a in (parents, lengths, groups, own, tree_kv, suffix_kv, shard, weight)]
    return pl.pallas_call(
        functools.partial(load_kernel, chunk_rows),
        in_specs=[pl.BlockSpec(memory_space=pltpu.HBM)] * 8,
        out_specs=[in_vmem()] * 7,
        out_shape=(
            jax.ShapeDtypeStruct((touched * node_count, node_count), jnp.float32),
            jax.ShapeDtypeStruct((touched, 8, suffix_kv.shape[1]), jnp.float32),
            jax.ShapeDtypeStruct((chunk_rows, own.shape[1]), own.dtype),
            jax.ShapeDtypeStruct((touched * node_count, tree_kv.shape[1]), tree_kv.dtype),
            jax.ShapeDtypeStruct((touched, *suffix_kv.shape[1:]), suffix_kv.dtype),
            jax.ShapeDtypeStruct(shard.shape, shard.dtype),
            jax.ShapeDtypeStruct(weight.shape, weight.dtype),
        ),
        scratch_shapes=[
            pltpu.VMEM(parents.shape, jnp.int32),
            pltpu.SMEM(lengths.shape, jnp.int32),
            pltpu.SMEM(groups.shape, jnp.int32),
            pltpu.SemaphoreType.DMA((8,)),
        ],
        compiler_params=pltpu.CompilerParams(vmem_limit_bytes=vmem_bytes),
        name="load",
        cost_estimate=pl.CostEstimate(flops=100_000_000, bytes_accessed=2_000_000, transcendentals=0),
    )(*sources)


def private(unit, chunk_rows, node_count, requests, loaded, other, parts):
    bias, notes, own, tree, suffix = loaded
    head_size = tree.shape[1] // 2
    state_rows = chunk_rows * 2 * (own.shape[1] // head_size)
    return pl.pallas_call(
        functools.partial(private_kernel, unit, chunk_rows, node_count, requests),
        in_specs=[in_vmem()] * (6 + len(parts)),
        out_specs=in_vmem(),
        out_shape=jax.ShapeDtypeStruct((state_rows, 4 * head_size), jnp.float32),
        compiler_params=pltpu.CompilerParams(vmem_limit_bytes=vmem_bytes),
        name="private",
        cost_estimate=pl.CostEstimate(flops=300_000_000, bytes_accessed=500_000, transcendentals=0),
    )(*loaded, other, *parts)


def far_kernel(unit, part_count, own_ref, other_ref, state_ref, *rest):
    parts, (weight_own_ref, weight_other_ref, out_ref, attended_ref) = rest[:part_count], rest[part_count:]
    chunk_rows = out_ref.shape[0]
    head_size = state_ref.shape[1] // 4
    rate = log2_rate(head_size)
    prompts = swapped_prompts(parts[0], parts[1], parts[0].shape[0] // fetches) if part_count == 2 else [parts[0][g] for g in range(parts[0].shape[0])]
    start = first_row(chunk_rows, 2)
    for number in range(chunk_rows // unit):
        row = pl.multiple_of(start + number * unit, unit)
        query = jnp.concatenate(
            [stacked_heads(own_ref, number * unit, unit, head_size), stacked_heads(other_ref, row, unit, head_size)], axis=0
        )
        rows = slice(number * query.shape[0], (number + 1) * query.shape[0])
        before, largest, total, group = (state_ref[rows, spot * head_size : (spot + 1) * head_size] for spot in range(4))
        prompt = prompt_of(prompts, jnp.concatenate([group[:1], group[:1]], axis=1))
        scores = score(query, prompt[:, :head_size])
        top = jnp.maximum(largest, jnp.max(scores, axis=1, keepdims=True))
        fade = jnp.exp2((largest - top) * rate)
        width = scores.shape[1] // head_size
        weight = jnp.exp2((scores - (top if width == 1 else jnp.concatenate([top] * width, axis=1))) * rate)
        total = total * fade + jnp.sum(weight, axis=1, keepdims=True)
        result = before * fade + jnp.dot(weight.astype(jnp.bfloat16), prompt[:, head_size:], preferred_element_type=jnp.float32)
        put_heads(attended_ref, number, unit, (result / total).astype(jnp.bfloat16))
    project(attended_ref, weight_own_ref, weight_other_ref, out_ref)


def near_kernel(
    unit, piece_count, length_ref, group_ref, own_ref, other_ref, parents_ref, accepted_ref, tree_ref, suffix_ref, *rest
):
    pieces, (weight_own_ref, weight_other_ref, out_ref, path_ref, attended_ref, bias_ref) = rest[:piece_count], rest[piece_count:]
    chunk_rows = out_ref.shape[0]
    requests, node_count = parents_ref.shape
    path_length = accepted_ref.shape[1]
    head_size = tree_ref.shape[1] // 2
    node = lax.broadcasted_iota(jnp.int32, (node_count, path_length), 0)
    for r, closure in enumerate(closures([parents_ref[r : r + 1, :] for r in range(requests)], node_count)):
        rows = slice(r * node_count, (r + 1) * node_count)
        bias_ref[rows, :] = bias_of(closure)
        chosen = jnp.broadcast_to(accepted_ref[r : r + 1, :], (node_count, path_length)) == node
        path_ref[r] = lax.dot_general(
            jnp.where(chosen, 1.0, 0.0).astype(jnp.bfloat16),
            tree_ref[rows, :],
            (((0,), (0,)), ((), ())),
            preferred_element_type=jnp.float32,
        ).astype(jnp.bfloat16)
    if piece_count == 3:
        kept = kept_prompts(pieces[0], pieces[1])
        prompts = [jnp.concatenate(pair, axis=0) for pair in zip(kept, swapped_prompts(pieces[1], pieces[2], len(kept)))]
    else:
        prompts = [pieces[0][g] for g in range(pieces[0].shape[0])]
    slot = lax.broadcasted_iota(jnp.int32, (1, suffix_ref.shape[1]), 1)
    start = first_row(chunk_rows, 0)
    for number in range(chunk_rows // unit):
        row = pl.multiple_of(start + number * unit, unit)
        query = jnp.concatenate([stacked_heads(ref, row, unit, head_size) for ref in (own_ref, other_ref)], axis=0)
        request = row // node_count
        used = jnp.where(slot < length_ref[request], 0.0, neg_large)
        tree = tree_ref[pl.ds(pl.multiple_of(request * node_count, node_count), node_count), :]
        blocks = private_blocks(query, bias_ref[pl.ds(row, unit), :], used, tree, suffix_ref[request])
        group = group_ref[request]
        prompt = prompt_of(prompts, group)
        blocks.append((score(query, prompt[:, :head_size]), prompt[:, head_size:]))
        largest, total, result = absorb(blocks, log2_rate(head_size))
        put_heads(attended_ref, number, unit, (result / total).astype(jnp.bfloat16))
    project(attended_ref, weight_own_ref, weight_other_ref, out_ref)


def chunk(kernel, name, outs, scalars, arrays, weights, scratch):
    return pl.pallas_call(
        kernel,
        in_specs=[in_smem()] * len(scalars) + [in_vmem()] * (len(arrays) + len(weights)),
        out_specs=[in_vmem()] * len(outs),
        out_shape=outs,
        scratch_shapes=[pltpu.VMEM((outs[0].shape[0], 2 * weights[0].shape[0]), jnp.bfloat16), *scratch],
        compiler_params=pltpu.CompilerParams(vmem_limit_bytes=vmem_bytes),
        name=name,
        cost_estimate=pl.CostEstimate(flops=500_000_000, bytes_accessed=1_000_000, transcendentals=0),
    )(*scalars, *arrays, *weights)


def local(req_count, tp_count, queries, tree_kv, suffix_kv, suffix_len, group_ids, parents, accepted, prompt_kv, out_weight):
    chunk_rows = queries.shape[0] // tp_count
    unit = math.gcd(chunk_rows, parents.shape[1])
    other_queries = swap_in_pair(queries, tp_count)
    if req_count == 8 and tp_count % 2 == 0:
        fetched = fetch_shards(prompt_kv, req_count, tp_count)
        other_weight = swap_in_pair(out_weight, tp_count)
    else:
        fetched = None
        other_weight = swap_in_pair(out_weight, tp_count)
    requests, node_count = parents.shape
    *loaded, shard, own_weight = load(unit, chunk_rows, parents, suffix_len, group_ids, queries, tree_kv, suffix_kv, prompt_kv, out_weight)
    if fetched is None:
        pieces = [lax.all_gather(prompt_kv, "req", axis=1, tiled=True)]
        state = private(unit, chunk_rows, node_count, requests, loaded, other_queries, [])
    else:
        joined = jnp.concatenate([after(piece, shard) for piece in fetched], axis=0)
        pieces = [shard, joined, swap_in_pair(joined, tp_count)]
        state = private(unit, chunk_rows, node_count, requests, loaded, other_queries, pieces[:2])
    parts = pieces[-2:]
    weights = (own_weight, other_weight)
    chunk_shape = (chunk_rows, out_weight.shape[1])
    (far,) = chunk(
        functools.partial(far_kernel, unit, len(parts)), "far_chunk", [jax.ShapeDtypeStruct(chunk_shape, jnp.bfloat16)],
        (), (loaded[2], other_queries, state, *parts), weights, ()
    )
    arrived = lax.ppermute(far, "tp", [(t, t ^ 2) for t in range(tp_count)])
    near, path_cache = chunk(
        functools.partial(near_kernel, unit, len(pieces)), "near_chunk",
        [jax.ShapeDtypeStruct(chunk_shape, jnp.float32), jax.ShapeDtypeStruct((*accepted.shape, tree_kv.shape[1]), jnp.bfloat16)],
        (suffix_len, group_ids), (queries, other_queries, parents, accepted, tree_kv, suffix_kv, *pieces), weights,
        (pltpu.VMEM((requests * node_count, node_count), jnp.float32),)
    )
    layer_output = (near + arrived.astype(jnp.float32)).astype(jnp.bfloat16)
    return (layer_output, path_cache)


def solution(mesh):
    return jax.shard_map(
        functools.partial(local, mesh.shape["req"], mesh.shape["tp"]),
        mesh=mesh,
        in_specs=(
            P("req", "tp"),
            P("req", None),
            P("req", None, None),
            P("req"),
            P("req"),
            P("req", None),
            P("req", None),
            P(None, "req", None),
            P("tp", None),
        ),
        out_specs=(P(("req", "tp"), None), P("req", None, None)),
        check_vma=False,
    )
```

```python
import functools
import math

import jax
import jax.numpy as jnp
from jax import lax
from jax.experimental import pallas as pl
from jax.experimental.pallas import tpu as pltpu
from jax.sharding import PartitionSpec as P

neg_large = -1e30
vmem_bytes = 12 * 1024 * 1024
fetches = 4


def fetch_shards(shard, req_count, tp_count):
    masks = ((7, 4, 3), (6, 5, 2, 1))
    arrived = []
    for step in range(fetches):
        pairs = []
        for r in range(req_count):
            for t in range(tp_count):
                mine = masks[t % 2]
                if step < len(mine):
                    pairs.append((r * tp_count + t, (r ^ mine[step]) * tp_count + t))
        arrived.append(lax.ppermute(shard, ("req", "tp"), pairs))
    return arrived


def touch_kernel(in_ref, out_ref):
    del in_ref, out_ref


def touched(array):
    return pl.pallas_call(
        touch_kernel,
        in_specs=[in_vmem()],
        out_specs=in_vmem(),
        out_shape=jax.ShapeDtypeStruct(array.shape, array.dtype),
        input_output_aliases={0: 0},
        compiler_params=pltpu.CompilerParams(vmem_limit_bytes=1024 * 1024),
        name="touch",
        cost_estimate=pl.CostEstimate(flops=int(5e9), bytes_accessed=0, transcendentals=0),
    )(array)


def after(array, earlier):
    return lax.optimization_barrier((array, earlier))[0]


def swap_in_pair(array, tp_count):
    return lax.ppermute(array, "tp", [(t, t ^ 1) for t in range(tp_count)])


def score(query, keys):
    return lax.dot_general(query, keys, (((1,), (1,)), ((), ())), preferred_element_type=jnp.float32)


def stacked_heads(ref, row, unit, head_size):
    return jnp.concatenate([ref[pl.ds(row, unit), h : h + head_size] for h in range(0, ref.shape[1], head_size)], axis=0)


def log2_rate(head_size):
    return head_size**-0.5 * math.log2(math.e)


def absorb(blocks, rate):
    largest = functools.reduce(jnp.maximum, [jnp.max(s, axis=1, keepdims=True) for s, _ in blocks])
    total, result = 0.0, 0.0
    for scores, values in blocks:
        weight = jnp.exp2((scores - largest) * rate)
        total = total + jnp.sum(weight, axis=1, keepdims=True)
        result = result + jnp.dot(weight.astype(jnp.bfloat16), values, preferred_element_type=jnp.float32)
    return largest, total, result


def private_blocks(query, bias, used, tree, suffix):
    head_size = query.shape[1]
    every = jnp.concatenate([bias] * (query.shape[0] // bias.shape[0]), axis=0)
    return [
        (score(query, tree[:, :head_size]) + every, tree[:, head_size:]),
        (score(query, suffix[:, :head_size]) + used, suffix[:, head_size:]),
    ]


def prompt_of(prompts, group):
    return functools.reduce(lambda held, g: jnp.where(group == g, prompts[g], held), range(1, len(prompts)), prompts[0])


def kept_prompts(shard, fetched):
    groups = shard.shape[0]
    return [jnp.concatenate([shard[g]] + [fetched[k + g] for k in range(0, fetched.shape[0] - groups, groups)], axis=0) for g in range(groups)]


def swapped_prompts(fetched, swapped, groups):
    last = swapped.shape[0] - groups
    return [jnp.concatenate([swapped[k + g] for k in range(0, last, groups)] + [fetched[last + g] + swapped[last + g]], axis=0) for g in range(groups)]


def project(attended_ref, weight_own_ref, weight_other_ref, out_ref, first=0):
    width = weight_own_ref.shape[0]
    count = out_ref.shape[1]
    columns = 512 if count % 512 == 0 else count
    for c in range(0, count, columns):
        product = jnp.dot(attended_ref[:, :width], weight_own_ref[:, first + c : first + c + columns], preferred_element_type=jnp.float32)
        product += jnp.dot(attended_ref[:, width:], weight_other_ref[:, first + c : first + c + columns], preferred_element_type=jnp.float32)
        out_ref[:, c : c + columns] = product.astype(out_ref.dtype)


def rest_kernel(first, attended_ref, weight_own_ref, weight_other_ref, out_ref):
    project(attended_ref, weight_own_ref, weight_other_ref, out_ref, first)


def sum_kernel(near_ref, *rest):
    *arrived, out_ref = rest
    first = 0
    for part_ref in arrived:
        columns = slice(first, first + part_ref.shape[1])
        out_ref[:, columns] = (near_ref[:, columns] + part_ref[...].astype(jnp.float32)).astype(out_ref.dtype)
        first += part_ref.shape[1]


def put_heads(attended_ref, number, unit, attended):
    head_size = attended.shape[1]
    for h in range(attended.shape[0] // unit):
        attended_ref[number * unit : (number + 1) * unit, h * head_size : (h + 1) * head_size] = attended[h * unit : (h + 1) * unit]


def first_row(chunk_rows, offset):
    return (lax.axis_index("tp") ^ offset) * chunk_rows


def closures(parents, node_count):
    above = lax.broadcasted_iota(jnp.int32, (node_count, node_count), 0)
    below = lax.broadcasted_iota(jnp.int32, (node_count, node_count), 1)
    found = []
    for parent in parents:
        step = ((jnp.broadcast_to(parent, (node_count, node_count)) == above) & (below > 0)) | (above == below)
        found.append(jnp.where(step, 1.0, 0.0).astype(jnp.bfloat16))
    for repeat in range(max(1, (node_count - 1).bit_length())):
        found = [jnp.dot(c, c, preferred_element_type=jnp.float32) for c in found]
        found = [jnp.where(c > 0.5, 1.0, 0.0).astype(jnp.bfloat16) for c in found]
    return found


def bias_of(closure):
    return jnp.where(closure.astype(jnp.float32).T > 0.5, 0.0, neg_large)


def first_request(chunk_rows, offset, node_count, requests, touched):
    return jnp.minimum(first_row(chunk_rows, offset) // node_count, requests - touched)


def load_kernel(
    chunk_rows, parents_hbm, length_hbm, group_hbm, own_hbm, tree_hbm, suffix_hbm, shard_hbm, weight_hbm,
    bias_ref, notes_ref, own_ref, tree_ref, suffix_ref, shard_ref, weight_ref, parents_ref, length_ref, group_ref, arrival
):
    requests, node_count = parents_ref.shape
    touched, slot_count = suffix_ref.shape[:2]
    start = pl.multiple_of(first_row(chunk_rows, 2), math.gcd(chunk_rows, node_count))
    base = first_request(chunk_rows, 2, node_count, requests, touched)
    copies = [
        pltpu.make_async_copy(source, target, arrival.at[place])
        for place, (source, target) in enumerate((
            (parents_hbm, parents_ref),
            (length_hbm, length_ref),
            (group_hbm, group_ref),
            (own_hbm.at[pl.ds(start, chunk_rows)], own_ref),
            (tree_hbm.at[pl.ds(pl.multiple_of(base * node_count, node_count), touched * node_count)], tree_ref),
            (suffix_hbm.at[pl.ds(base, touched)], suffix_ref),
            (shard_hbm, shard_ref),
            (weight_hbm, weight_ref),
        ))
    ]
    for copy in copies:
        copy.start()
    for copy in copies[:3]:
        copy.wait()
    found = closures([parents_ref[pl.ds(base + k, 1), :] for k in range(touched)], node_count)
    slot = lax.broadcasted_iota(jnp.int32, (1, slot_count), 1)
    for k in range(touched):
        bias_ref[k * node_count : (k + 1) * node_count, :] = bias_of(found[k])
        notes_ref[k, :1, :] = jnp.where(slot < length_ref[base + k], 0.0, neg_large)
        notes_ref[k, 1:2, :] = jnp.broadcast_to(group_ref[base + k].astype(jnp.float32), (1, slot_count))
    for copy in copies[3:]:
        copy.wait()


def private_kernel(unit, chunk_rows, node_count, requests, bias_ref, notes_ref, own_ref, tree_ref, suffix_ref, other_ref, *rest):
    head_size = tree_ref.shape[1] // 2
    touched = suffix_ref.shape[0]
    *parts, state_ref = rest
    prompts = kept_prompts(*parts) if parts else []
    start = pl.multiple_of(first_row(chunk_rows, 2), unit)
    base = first_request(chunk_rows, 2, node_count, requests, touched)
    for number in range(chunk_rows // unit):
        row = pl.multiple_of(start + number * unit, unit)
        place = row // node_count - base
        query = jnp.concatenate(
            [stacked_heads(own_ref, number * unit, unit, head_size), stacked_heads(other_ref, row, unit, head_size)], axis=0
        )
        bias = bias_ref[pl.ds(pl.multiple_of(row - base * node_count, unit), unit), :]
        tree = tree_ref[pl.ds(pl.multiple_of(place * node_count, node_count), node_count), :]
        notes = notes_ref[place]
        group = notes[1:2]
        blocks = private_blocks(query, bias, notes[:1], tree, suffix_ref[place])
        if prompts:
            prompt = prompt_of(prompts, group[:, : 2 * head_size])
            blocks.append((score(query, prompt[:, :head_size]), prompt[:, head_size:]))
        largest, total, result = absorb(blocks, log2_rate(head_size))
        lanes = result.shape
        rows = slice(number * lanes[0], (number + 1) * lanes[0])
        for spot, value in enumerate((result, largest, total, group[:, :head_size])):
            state_ref[rows, spot * head_size : (spot + 1) * head_size] = jnp.broadcast_to(value, lanes)


def in_smem():
    return pl.BlockSpec(memory_space=pltpu.SMEM)


def in_vmem():
    return pl.BlockSpec(memory_space=pltpu.VMEM)


def load(unit, chunk_rows, parents, lengths, groups, own, tree_kv, suffix_kv, shard, weight):
    requests, node_count = parents.shape
    touched = min(requests, -(-(chunk_rows + node_count - unit) // node_count))
    sources = [pltpu.with_memory_space_constraint(a, pltpu.HBM) for a in (parents, lengths, groups, own, tree_kv, suffix_kv, shard, weight)]
    return pl.pallas_call(
        functools.partial(load_kernel, chunk_rows),
        in_specs=[pl.BlockSpec(memory_space=pltpu.HBM)] * 8,
        out_specs=[in_vmem()] * 7,
        out_shape=(
            jax.ShapeDtypeStruct((touched * node_count, node_count), jnp.float32),
            jax.ShapeDtypeStruct((touched, 8, suffix_kv.shape[1]), jnp.float32),
            jax.ShapeDtypeStruct((chunk_rows, own.shape[1]), own.dtype),
            jax.ShapeDtypeStruct((touched * node_count, tree_kv.shape[1]), tree_kv.dtype),
            jax.ShapeDtypeStruct((touched, *suffix_kv.shape[1:]), suffix_kv.dtype),
            jax.ShapeDtypeStruct(shard.shape, shard.dtype),
            jax.ShapeDtypeStruct(weight.shape, weight.dtype),
        ),
        scratch_shapes=[
            pltpu.VMEM(parents.shape, jnp.int32),
            pltpu.SMEM(lengths.shape, jnp.int32),
            pltpu.SMEM(groups.shape, jnp.int32),
            pltpu.SemaphoreType.DMA((8,)),
        ],
        compiler_params=pltpu.CompilerParams(vmem_limit_bytes=vmem_bytes),
        name="load",
        cost_estimate=pl.CostEstimate(flops=100_000_000, bytes_accessed=2_000_000, transcendentals=0),
    )(*sources)


def private(unit, chunk_rows, node_count, requests, loaded, other, parts):
    bias, notes, own, tree, suffix = loaded
    head_size = tree.shape[1] // 2
    state_rows = chunk_rows * 2 * (own.shape[1] // head_size)
    return pl.pallas_call(
        functools.partial(private_kernel, unit, chunk_rows, node_count, requests),
        in_specs=[in_vmem()] * (6 + len(parts)),
        out_specs=in_vmem(),
        out_shape=jax.ShapeDtypeStruct((state_rows, 4 * head_size), jnp.float32),
        compiler_params=pltpu.CompilerParams(vmem_limit_bytes=vmem_bytes),
        name="private",
        cost_estimate=pl.CostEstimate(flops=300_000_000, bytes_accessed=500_000, transcendentals=0),
    )(*loaded, other, *parts)


def far_kernel(unit, part_count, own_ref, other_ref, state_ref, *rest):
    parts, (weight_own_ref, weight_other_ref, out_ref, attended_ref) = rest[:part_count], rest[part_count:]
    chunk_rows = out_ref.shape[0]
    head_size = state_ref.shape[1] // 4
    rate = log2_rate(head_size)
    prompts = swapped_prompts(parts[0], parts[1], parts[0].shape[0] // fetches) if part_count == 2 else [parts[0][g] for g in range(parts[0].shape[0])]
    start = first_row(chunk_rows, 2)
    for number in range(chunk_rows // unit):
        row = pl.multiple_of(start + number * unit, unit)
        query = jnp.concatenate(
            [stacked_heads(own_ref, number * unit, unit, head_size), stacked_heads(other_ref, row, unit, head_size)], axis=0
        )
        rows = slice(number * query.shape[0], (number + 1) * query.shape[0])
        before, largest, total, group = (state_ref[rows, spot * head_size : (spot + 1) * head_size] for spot in range(4))
        prompt = prompt_of(prompts, jnp.concatenate([group[:1], group[:1]], axis=1))
        scores = score(query, prompt[:, :head_size])
        top = jnp.maximum(largest, jnp.max(scores, axis=1, keepdims=True))
        fade = jnp.exp2((largest - top) * rate)
        width = scores.shape[1] // head_size
        weight = jnp.exp2((scores - (top if width == 1 else jnp.concatenate([top] * width, axis=1))) * rate)
        total = total * fade + jnp.sum(weight, axis=1, keepdims=True)
        result = before * fade + jnp.dot(weight.astype(jnp.bfloat16), prompt[:, head_size:], preferred_element_type=jnp.float32)
        put_heads(attended_ref, number, unit, (result / total).astype(jnp.bfloat16))
    project(attended_ref, weight_own_ref, weight_other_ref, out_ref)


def near_kernel(
    unit, piece_count, length_ref, group_ref, own_ref, other_ref, parents_ref, accepted_ref, tree_ref, suffix_ref, *rest
):
    pieces, (weight_own_ref, weight_other_ref, out_ref, path_ref, attended_ref, bias_ref) = rest[:piece_count], rest[piece_count:]
    chunk_rows = out_ref.shape[0]
    requests, node_count = parents_ref.shape
    path_length = accepted_ref.shape[1]
    head_size = tree_ref.shape[1] // 2
    node = lax.broadcasted_iota(jnp.int32, (node_count, path_length), 0)
    for r, closure in enumerate(closures([parents_ref[r : r + 1, :] for r in range(requests)], node_count)):
        rows = slice(r * node_count, (r + 1) * node_count)
        bias_ref[rows, :] = bias_of(closure)
        chosen = jnp.broadcast_to(accepted_ref[r : r + 1, :], (node_count, path_length)) == node
        path_ref[r] = lax.dot_general(
            jnp.where(chosen, 1.0, 0.0).astype(jnp.bfloat16),
            tree_ref[rows, :],
            (((0,), (0,)), ((), ())),
            preferred_element_type=jnp.float32,
        ).astype(jnp.bfloat16)
    if piece_count == 3:
        kept = kept_prompts(pieces[0], pieces[1])
        prompts = [jnp.concatenate(pair, axis=0) for pair in zip(kept, swapped_prompts(pieces[1], pieces[2], len(kept)))]
    else:
        prompts = [pieces[0][g] for g in range(pieces[0].shape[0])]
    slot = lax.broadcasted_iota(jnp.int32, (1, suffix_ref.shape[1]), 1)
    start = first_row(chunk_rows, 0)
    for number in range(chunk_rows // unit):
        row = pl.multiple_of(start + number * unit, unit)
        query = jnp.concatenate([stacked_heads(ref, row, unit, head_size) for ref in (own_ref, other_ref)], axis=0)
        request = row // node_count
        used = jnp.where(slot < length_ref[request], 0.0, neg_large)
        tree = tree_ref[pl.ds(pl.multiple_of(request * node_count, node_count), node_count), :]
        blocks = private_blocks(query, bias_ref[pl.ds(row, unit), :], used, tree, suffix_ref[request])
        group = group_ref[request]
        prompt = prompt_of(prompts, group)
        blocks.append((score(query, prompt[:, :head_size]), prompt[:, head_size:]))
        largest, total, result = absorb(blocks, log2_rate(head_size))
        put_heads(attended_ref, number, unit, (result / total).astype(jnp.bfloat16))
    project(attended_ref, weight_own_ref, weight_other_ref, out_ref)


def chunk(kernel, name, outs, scalars, arrays, weights, scratch=(), flops=500_000_000):
    return pl.pallas_call(
        kernel,
        in_specs=[in_smem()] * len(scalars) + [in_vmem()] * (len(arrays) + len(weights)),
        out_specs=[in_vmem()] * len(outs),
        out_shape=outs,
        scratch_shapes=scratch,
        compiler_params=pltpu.CompilerParams(vmem_limit_bytes=vmem_bytes),
        name=name,
        cost_estimate=pl.CostEstimate(flops=flops, bytes_accessed=1_000_000, transcendentals=0),
    )(*scalars, *arrays, *weights)


def local(req_count, tp_count, queries, tree_kv, suffix_kv, suffix_len, group_ids, parents, accepted, prompt_kv, out_weight):
    chunk_rows = queries.shape[0] // tp_count
    unit = math.gcd(chunk_rows, parents.shape[1])
    other_queries = swap_in_pair(queries, tp_count)
    if req_count == 8 and tp_count % 2 == 0:
        fetched = fetch_shards(prompt_kv, req_count, tp_count)
        other_weight = swap_in_pair(out_weight, tp_count)
    else:
        fetched = None
        other_weight = swap_in_pair(out_weight, tp_count)
    requests, node_count = parents.shape
    *loaded, shard, own_weight = load(unit, chunk_rows, parents, suffix_len, group_ids, queries, tree_kv, suffix_kv, prompt_kv, out_weight)
    if fetched is None:
        pieces = [lax.all_gather(prompt_kv, "req", axis=1, tiled=True)]
        state = private(unit, chunk_rows, node_count, requests, loaded, other_queries, [])
    else:
        joined = jnp.concatenate([after(piece, shard) for piece in fetched], axis=0)
        pieces = [shard, joined, swap_in_pair(joined, tp_count)]
        state = private(unit, chunk_rows, node_count, requests, loaded, other_queries, pieces[:2])
    parts = pieces[-2:]
    weights = (own_weight, other_weight)
    columns = out_weight.shape[1]
    early = columns // 4
    attended_shape = (chunk_rows, 2 * out_weight.shape[0])
    early_far, attended = chunk(
        functools.partial(far_kernel, unit, len(parts)), "far_chunk",
        [jax.ShapeDtypeStruct((chunk_rows, early), jnp.bfloat16), jax.ShapeDtypeStruct(attended_shape, jnp.bfloat16)],
        (), (loaded[2], other_queries, state, *parts), weights, flops=200_000_000
    )
    across = [(t, t ^ 2) for t in range(tp_count)]
    early_arrived = touched(lax.ppermute(early_far, "tp", across))
    (late_far,) = chunk(
        functools.partial(rest_kernel, early), "far_rest", [jax.ShapeDtypeStruct((chunk_rows, columns - early), jnp.bfloat16)],
        (), (attended,), weights, flops=300_000_000
    )
    late_arrived = lax.ppermute(late_far, "tp", across)
    near, path_cache = chunk(
        functools.partial(near_kernel, unit, len(pieces)), "near_chunk",
        [jax.ShapeDtypeStruct((chunk_rows, columns), jnp.float32), jax.ShapeDtypeStruct((*accepted.shape, tree_kv.shape[1]), jnp.bfloat16)],
        (suffix_len, group_ids), (queries, other_queries, parents, accepted, tree_kv, suffix_kv, *pieces), weights,
        (pltpu.VMEM(attended_shape, jnp.bfloat16), pltpu.VMEM((requests * node_count, node_count), jnp.float32))
    )
    (layer_output,) = chunk(
        sum_kernel, "sum", [jax.ShapeDtypeStruct((chunk_rows, columns), jnp.bfloat16)], (), (near, early_arrived, late_arrived), (), flops=1_000_000
    )
    return (layer_output, path_cache)


def solution(mesh):
    return jax.shard_map(
        functools.partial(local, mesh.shape["req"], mesh.shape["tp"]),
        mesh=mesh,
        in_specs=(
            P("req", "tp"),
            P("req", None),
            P("req", None, None),
            P("req"),
            P("req"),
            P("req", None),
            P("req", None),
            P(None, "req", None),
            P("tp", None),
        ),
        out_specs=(P(("req", "tp"), None), P("req", None, None)),
        check_vma=False,
    )
```

```python
import functools
import math

import jax
import jax.numpy as jnp
from jax import lax
from jax.experimental import pallas as pl
from jax.experimental.pallas import tpu as pltpu
from jax.sharding import PartitionSpec as P

neg_large = -1e30
vmem_bytes = 12 * 1024 * 1024
fetches = 4


def fetch_shards(shard, req_count, tp_count):
    masks = ((4, 5, 3), (6, 7, 2, 1))
    arrived = []
    for step in range(fetches):
        pairs = []
        for r in range(req_count):
            for t in range(tp_count):
                mine = masks[t % 2]
                if step < len(mine):
                    pairs.append((r * tp_count + t, (r ^ mine[step]) * tp_count + t))
        arrived.append(lax.ppermute(shard, ("req", "tp"), pairs))
    return arrived


def touch_kernel(in_ref, out_ref):
    del in_ref, out_ref


def touched(array):
    return pl.pallas_call(
        touch_kernel,
        in_specs=[in_vmem()],
        out_specs=in_vmem(),
        out_shape=jax.ShapeDtypeStruct(array.shape, array.dtype),
        input_output_aliases={0: 0},
        compiler_params=pltpu.CompilerParams(vmem_limit_bytes=1024 * 1024),
        name="touch",
        cost_estimate=pl.CostEstimate(flops=int(5e9), bytes_accessed=0, transcendentals=0),
    )(array)


def after(array, earlier):
    return lax.optimization_barrier((array, earlier))[0]


def swap_in_pair(array, tp_count):
    return lax.ppermute(array, "tp", [(t, t ^ 1) for t in range(tp_count)])


def score(query, keys):
    return lax.dot_general(query, keys, (((1,), (1,)), ((), ())), preferred_element_type=jnp.float32)


def stacked_heads(ref, row, unit, head_size):
    return jnp.concatenate([ref[pl.ds(row, unit), h : h + head_size] for h in range(0, ref.shape[1], head_size)], axis=0)


def log2_rate(head_size):
    return head_size**-0.5 * math.log2(math.e)


def absorb(blocks, rate):
    largest = functools.reduce(jnp.maximum, [jnp.max(s, axis=1, keepdims=True) for s, _ in blocks])
    total, result = 0.0, 0.0
    for scores, values in blocks:
        weight = jnp.exp2((scores - largest) * rate)
        total = total + jnp.sum(weight, axis=1, keepdims=True)
        result = result + jnp.dot(weight.astype(jnp.bfloat16), values, preferred_element_type=jnp.float32)
    return largest, total, result


def private_blocks(query, bias, used, tree, suffix):
    head_size = query.shape[1]
    every = jnp.concatenate([bias] * (query.shape[0] // bias.shape[0]), axis=0)
    return [
        (score(query, tree[:, :head_size]) + every, tree[:, head_size:]),
        (score(query, suffix[:, :head_size]) + used, suffix[:, head_size:]),
    ]


def prompt_of(prompts, group):
    return functools.reduce(lambda held, g: jnp.where(group == g, prompts[g], held), range(1, len(prompts)), prompts[0])


def kept_prompts(shard, fetched):
    groups = shard.shape[0]
    return [jnp.concatenate([shard[g]] + [fetched[k + g] for k in range(0, fetched.shape[0] - groups, groups)], axis=0) for g in range(groups)]


def swapped_prompts(fetched, swapped, groups):
    last = swapped.shape[0] - groups
    return [jnp.concatenate([swapped[k + g] for k in range(0, last, groups)] + [fetched[last + g] + swapped[last + g]], axis=0) for g in range(groups)]


def project(attended_ref, weight_own_ref, weight_other_ref, out_ref, first=0):
    width = weight_own_ref.shape[0]
    count = out_ref.shape[1]
    columns = 512 if count % 512 == 0 else count
    for c in range(0, count, columns):
        product = jnp.dot(attended_ref[:, :width], weight_own_ref[:, first + c : first + c + columns], preferred_element_type=jnp.float32)
        product += jnp.dot(attended_ref[:, width:], weight_other_ref[:, first + c : first + c + columns], preferred_element_type=jnp.float32)
        out_ref[:, c : c + columns] = product.astype(out_ref.dtype)


def rest_kernel(first, attended_ref, weight_own_ref, weight_other_ref, out_ref):
    project(attended_ref, weight_own_ref, weight_other_ref, out_ref, first)


def sum_kernel(near_ref, *rest):
    *arrived, out_ref = rest
    first = 0
    for part_ref in arrived:
        columns = slice(first, first + part_ref.shape[1])
        out_ref[:, columns] = (near_ref[:, columns] + part_ref[...].astype(jnp.float32)).astype(out_ref.dtype)
        first += part_ref.shape[1]


def put_heads(attended_ref, number, unit, attended):
    head_size = attended.shape[1]
    for h in range(attended.shape[0] // unit):
        attended_ref[number * unit : (number + 1) * unit, h * head_size : (h + 1) * head_size] = attended[h * unit : (h + 1) * unit]


def first_row(chunk_rows, offset):
    return (lax.axis_index("tp") ^ offset) * chunk_rows


def closures(parents, node_count):
    above = lax.broadcasted_iota(jnp.int32, (node_count, node_count), 0)
    below = lax.broadcasted_iota(jnp.int32, (node_count, node_count), 1)
    found = []
    for parent in parents:
        step = ((jnp.broadcast_to(parent, (node_count, node_count)) == above) & (below > 0)) | (above == below)
        found.append(jnp.where(step, 1.0, 0.0).astype(jnp.bfloat16))
    for repeat in range(max(1, (node_count - 1).bit_length())):
        found = [jnp.dot(c, c, preferred_element_type=jnp.float32) for c in found]
        found = [jnp.where(c > 0.5, 1.0, 0.0).astype(jnp.bfloat16) for c in found]
    return found


def bias_of(closure):
    return jnp.where(closure.astype(jnp.float32).T > 0.5, 0.0, neg_large)


def first_request(chunk_rows, offset, node_count, requests, touched):
    return jnp.minimum(first_row(chunk_rows, offset) // node_count, requests - touched)


def load_kernel(
    chunk_rows, parents_hbm, length_hbm, group_hbm, own_hbm, tree_hbm, suffix_hbm, shard_hbm, weight_hbm,
    bias_ref, notes_ref, own_ref, tree_ref, suffix_ref, shard_ref, weight_ref, parents_ref, length_ref, group_ref, arrival
):
    requests, node_count = parents_ref.shape
    touched, slot_count = suffix_ref.shape[:2]
    start = pl.multiple_of(first_row(chunk_rows, 2), math.gcd(chunk_rows, node_count))
    base = first_request(chunk_rows, 2, node_count, requests, touched)
    copies = [
        pltpu.make_async_copy(source, target, arrival.at[place])
        for place, (source, target) in enumerate((
            (parents_hbm, parents_ref),
            (length_hbm, length_ref),
            (group_hbm, group_ref),
            (own_hbm.at[pl.ds(start, chunk_rows)], own_ref),
            (tree_hbm.at[pl.ds(pl.multiple_of(base * node_count, node_count), touched * node_count)], tree_ref),
            (suffix_hbm.at[pl.ds(base, touched)], suffix_ref),
            (shard_hbm, shard_ref),
            (weight_hbm, weight_ref),
        ))
    ]
    for copy in copies:
        copy.start()
    for copy in copies[:3]:
        copy.wait()
    found = closures([parents_ref[pl.ds(base + k, 1), :] for k in range(touched)], node_count)
    slot = lax.broadcasted_iota(jnp.int32, (1, slot_count), 1)
    for k in range(touched):
        bias_ref[k * node_count : (k + 1) * node_count, :] = bias_of(found[k])
        notes_ref[k, :1, :] = jnp.where(slot < length_ref[base + k], 0.0, neg_large)
        notes_ref[k, 1:2, :] = jnp.broadcast_to(group_ref[base + k].astype(jnp.float32), (1, slot_count))
    for copy in copies[3:]:
        copy.wait()


def private_kernel(unit, chunk_rows, node_count, requests, bias_ref, notes_ref, own_ref, tree_ref, suffix_ref, other_ref, *rest):
    head_size = tree_ref.shape[1] // 2
    touched = suffix_ref.shape[0]
    *parts, state_ref = rest
    prompts = kept_prompts(*parts) if parts else []
    start = pl.multiple_of(first_row(chunk_rows, 2), unit)
    base = first_request(chunk_rows, 2, node_count, requests, touched)
    for number in range(chunk_rows // unit):
        row = pl.multiple_of(start + number * unit, unit)
        place = row // node_count - base
        query = jnp.concatenate(
            [stacked_heads(own_ref, number * unit, unit, head_size), stacked_heads(other_ref, row, unit, head_size)], axis=0
        )
        bias = bias_ref[pl.ds(pl.multiple_of(row - base * node_count, unit), unit), :]
        tree = tree_ref[pl.ds(pl.multiple_of(place * node_count, node_count), node_count), :]
        notes = notes_ref[place]
        group = notes[1:2]
        blocks = private_blocks(query, bias, notes[:1], tree, suffix_ref[place])
        if prompts:
            prompt = prompt_of(prompts, group[:, : 2 * head_size])
            blocks.append((score(query, prompt[:, :head_size]), prompt[:, head_size:]))
        largest, total, result = absorb(blocks, log2_rate(head_size))
        lanes = result.shape
        rows = slice(number * lanes[0], (number + 1) * lanes[0])
        for spot, value in enumerate((result, largest, total, group[:, :head_size])):
            state_ref[rows, spot * head_size : (spot + 1) * head_size] = jnp.broadcast_to(value, lanes)


def in_smem():
    return pl.BlockSpec(memory_space=pltpu.SMEM)


def in_vmem():
    return pl.BlockSpec(memory_space=pltpu.VMEM)


def load(unit, chunk_rows, parents, lengths, groups, own, tree_kv, suffix_kv, shard, weight):
    requests, node_count = parents.shape
    touched = min(requests, -(-(chunk_rows + node_count - unit) // node_count))
    sources = [pltpu.with_memory_space_constraint(a, pltpu.HBM) for a in (parents, lengths, groups, own, tree_kv, suffix_kv, shard, weight)]
    return pl.pallas_call(
        functools.partial(load_kernel, chunk_rows),
        in_specs=[pl.BlockSpec(memory_space=pltpu.HBM)] * 8,
        out_specs=[in_vmem()] * 7,
        out_shape=(
            jax.ShapeDtypeStruct((touched * node_count, node_count), jnp.float32),
            jax.ShapeDtypeStruct((touched, 8, suffix_kv.shape[1]), jnp.float32),
            jax.ShapeDtypeStruct((chunk_rows, own.shape[1]), own.dtype),
            jax.ShapeDtypeStruct((touched * node_count, tree_kv.shape[1]), tree_kv.dtype),
            jax.ShapeDtypeStruct((touched, *suffix_kv.shape[1:]), suffix_kv.dtype),
            jax.ShapeDtypeStruct(shard.shape, shard.dtype),
            jax.ShapeDtypeStruct(weight.shape, weight.dtype),
        ),
        scratch_shapes=[
            pltpu.VMEM(parents.shape, jnp.int32),
            pltpu.SMEM(lengths.shape, jnp.int32),
            pltpu.SMEM(groups.shape, jnp.int32),
            pltpu.SemaphoreType.DMA((8,)),
        ],
        compiler_params=pltpu.CompilerParams(vmem_limit_bytes=vmem_bytes),
        name="load",
        cost_estimate=pl.CostEstimate(flops=100_000_000, bytes_accessed=2_000_000, transcendentals=0),
    )(*sources)


def private(unit, chunk_rows, node_count, requests, loaded, other, parts):
    bias, notes, own, tree, suffix = loaded
    head_size = tree.shape[1] // 2
    state_rows = chunk_rows * 2 * (own.shape[1] // head_size)
    return pl.pallas_call(
        functools.partial(private_kernel, unit, chunk_rows, node_count, requests),
        in_specs=[in_vmem()] * (6 + len(parts)),
        out_specs=in_vmem(),
        out_shape=jax.ShapeDtypeStruct((state_rows, 4 * head_size), jnp.float32),
        compiler_params=pltpu.CompilerParams(vmem_limit_bytes=vmem_bytes),
        name="private",
        cost_estimate=pl.CostEstimate(flops=300_000_000, bytes_accessed=500_000, transcendentals=0),
    )(*loaded, other, *parts)


def far_kernel(unit, part_count, own_ref, other_ref, state_ref, *rest):
    parts, (weight_own_ref, weight_other_ref, out_ref, attended_ref) = rest[:part_count], rest[part_count:]
    chunk_rows = out_ref.shape[0]
    head_size = state_ref.shape[1] // 4
    rate = log2_rate(head_size)
    prompts = swapped_prompts(parts[0], parts[1], parts[0].shape[0] // fetches) if part_count == 2 else [parts[0][g] for g in range(parts[0].shape[0])]
    start = first_row(chunk_rows, 2)
    for number in range(chunk_rows // unit):
        row = pl.multiple_of(start + number * unit, unit)
        query = jnp.concatenate(
            [stacked_heads(own_ref, number * unit, unit, head_size), stacked_heads(other_ref, row, unit, head_size)], axis=0
        )
        rows = slice(number * query.shape[0], (number + 1) * query.shape[0])
        before, largest, total, group = (state_ref[rows, spot * head_size : (spot + 1) * head_size] for spot in range(4))
        prompt = prompt_of(prompts, jnp.concatenate([group[:1], group[:1]], axis=1))
        scores = score(query, prompt[:, :head_size])
        top = jnp.maximum(largest, jnp.max(scores, axis=1, keepdims=True))
        fade = jnp.exp2((largest - top) * rate)
        width = scores.shape[1] // head_size
        weight = jnp.exp2((scores - (top if width == 1 else jnp.concatenate([top] * width, axis=1))) * rate)
        total = total * fade + jnp.sum(weight, axis=1, keepdims=True)
        result = before * fade + jnp.dot(weight.astype(jnp.bfloat16), prompt[:, head_size:], preferred_element_type=jnp.float32)
        put_heads(attended_ref, number, unit, (result / total).astype(jnp.bfloat16))
    project(attended_ref, weight_own_ref, weight_other_ref, out_ref)


def near_kernel(
    unit, piece_count, length_ref, group_ref, own_ref, other_ref, parents_ref, accepted_ref, tree_ref, suffix_ref, *rest
):
    pieces, (weight_own_ref, weight_other_ref, out_ref, path_ref, attended_ref, bias_ref) = rest[:piece_count], rest[piece_count:]
    chunk_rows = out_ref.shape[0]
    requests, node_count = parents_ref.shape
    path_length = accepted_ref.shape[1]
    head_size = tree_ref.shape[1] // 2
    node = lax.broadcasted_iota(jnp.int32, (node_count, path_length), 0)
    for r, closure in enumerate(closures([parents_ref[r : r + 1, :] for r in range(requests)], node_count)):
        rows = slice(r * node_count, (r + 1) * node_count)
        bias_ref[rows, :] = bias_of(closure)
        chosen = jnp.broadcast_to(accepted_ref[r : r + 1, :], (node_count, path_length)) == node
        path_ref[r] = lax.dot_general(
            jnp.where(chosen, 1.0, 0.0).astype(jnp.bfloat16),
            tree_ref[rows, :],
            (((0,), (0,)), ((), ())),
            preferred_element_type=jnp.float32,
        ).astype(jnp.bfloat16)
    if piece_count == 3:
        kept = kept_prompts(pieces[0], pieces[1])
        prompts = [jnp.concatenate(pair, axis=0) for pair in zip(kept, swapped_prompts(pieces[1], pieces[2], len(kept)))]
    else:
        prompts = [pieces[0][g] for g in range(pieces[0].shape[0])]
    slot = lax.broadcasted_iota(jnp.int32, (1, suffix_ref.shape[1]), 1)
    start = first_row(chunk_rows, 0)
    for number in range(chunk_rows // unit):
        row = pl.multiple_of(start + number * unit, unit)
        query = jnp.concatenate([stacked_heads(ref, row, unit, head_size) for ref in (own_ref, other_ref)], axis=0)
        request = row // node_count
        used = jnp.where(slot < length_ref[request], 0.0, neg_large)
        tree = tree_ref[pl.ds(pl.multiple_of(request * node_count, node_count), node_count), :]
        blocks = private_blocks(query, bias_ref[pl.ds(row, unit), :], used, tree, suffix_ref[request])
        group = group_ref[request]
        prompt = prompt_of(prompts, group)
        blocks.append((score(query, prompt[:, :head_size]), prompt[:, head_size:]))
        largest, total, result = absorb(blocks, log2_rate(head_size))
        put_heads(attended_ref, number, unit, (result / total).astype(jnp.bfloat16))
    project(attended_ref, weight_own_ref, weight_other_ref, out_ref)


def chunk(kernel, name, outs, scalars, arrays, weights, scratch=(), flops=500_000_000):
    return pl.pallas_call(
        kernel,
        in_specs=[in_smem()] * len(scalars) + [in_vmem()] * (len(arrays) + len(weights)),
        out_specs=[in_vmem()] * len(outs),
        out_shape=outs,
        scratch_shapes=scratch,
        compiler_params=pltpu.CompilerParams(vmem_limit_bytes=vmem_bytes),
        name=name,
        cost_estimate=pl.CostEstimate(flops=flops, bytes_accessed=1_000_000, transcendentals=0),
    )(*scalars, *arrays, *weights)


def local(req_count, tp_count, queries, tree_kv, suffix_kv, suffix_len, group_ids, parents, accepted, prompt_kv, out_weight):
    chunk_rows = queries.shape[0] // tp_count
    unit = math.gcd(chunk_rows, parents.shape[1])
    other_queries = swap_in_pair(queries, tp_count)
    if req_count == 8 and tp_count % 2 == 0:
        fetched = fetch_shards(prompt_kv, req_count, tp_count)
        other_weight = swap_in_pair(out_weight, tp_count)
    else:
        fetched = None
        other_weight = swap_in_pair(out_weight, tp_count)
    requests, node_count = parents.shape
    *loaded, shard, own_weight = load(unit, chunk_rows, parents, suffix_len, group_ids, queries, tree_kv, suffix_kv, prompt_kv, out_weight)
    if fetched is None:
        pieces = [lax.all_gather(prompt_kv, "req", axis=1, tiled=True)]
        state = private(unit, chunk_rows, node_count, requests, loaded, other_queries, [])
    else:
        joined = jnp.concatenate([after(piece, shard) for piece in fetched], axis=0)
        pieces = [shard, joined, swap_in_pair(joined, tp_count)]
        state = private(unit, chunk_rows, node_count, requests, loaded, other_queries, pieces[:2])
    parts = pieces[-2:]
    weights = (own_weight, other_weight)
    columns = out_weight.shape[1]
    early = columns // 4
    attended_shape = (chunk_rows, 2 * out_weight.shape[0])
    early_far, attended = chunk(
        functools.partial(far_kernel, unit, len(parts)), "far_chunk",
        [jax.ShapeDtypeStruct((chunk_rows, early), jnp.bfloat16), jax.ShapeDtypeStruct(attended_shape, jnp.bfloat16)],
        (), (loaded[2], other_queries, state, *parts), weights, flops=200_000_000
    )
    across = [(t, t ^ 2) for t in range(tp_count)]
    early_arrived = touched(lax.ppermute(early_far, "tp", across))
    (late_far,) = chunk(
        functools.partial(rest_kernel, early), "far_rest", [jax.ShapeDtypeStruct((chunk_rows, columns - early), jnp.bfloat16)],
        (), (attended,), weights, flops=300_000_000
    )
    late_arrived = lax.ppermute(late_far, "tp", across)
    near, path_cache = chunk(
        functools.partial(near_kernel, unit, len(pieces)), "near_chunk",
        [jax.ShapeDtypeStruct((chunk_rows, columns), jnp.float32), jax.ShapeDtypeStruct((*accepted.shape, tree_kv.shape[1]), jnp.bfloat16)],
        (suffix_len, group_ids), (queries, other_queries, parents, accepted, tree_kv, suffix_kv, *pieces), weights,
        (pltpu.VMEM(attended_shape, jnp.bfloat16), pltpu.VMEM((requests * node_count, node_count), jnp.float32))
    )
    (layer_output,) = chunk(
        sum_kernel, "sum", [jax.ShapeDtypeStruct((chunk_rows, columns), jnp.bfloat16)], (), (near, early_arrived, late_arrived), (), flops=1_000_000
    )
    return (layer_output, path_cache)


def solution(mesh):
    return jax.shard_map(
        functools.partial(local, mesh.shape["req"], mesh.shape["tp"]),
        mesh=mesh,
        in_specs=(
            P("req", "tp"),
            P("req", None),
            P("req", None, None),
            P("req"),
            P("req"),
            P("req", None),
            P("req", None),
            P(None, "req", None),
            P("tp", None),
        ),
        out_specs=(P(("req", "tp"), None), P("req", None, None)),
        check_vma=False,
    )
```

```python
import functools
import math

import jax
import jax.numpy as jnp
from jax import lax
from jax.experimental import pallas as pl
from jax.experimental.pallas import tpu as pltpu
from jax.sharding import PartitionSpec as P

neg_large = -1e30
vmem_bytes = 12 * 1024 * 1024
fetches = 4


def fetch_shards(shard, req_count, tp_count):
    masks = ((4, 5, 3), (6, 7, 2, 1))
    arrived = []
    for step in range(fetches):
        pairs = []
        for r in range(req_count):
            for t in range(tp_count):
                mine = masks[t % 2]
                if step < len(mine):
                    pairs.append((r * tp_count + t, (r ^ mine[step]) * tp_count + t))
        arrived.append(lax.ppermute(shard, ("req", "tp"), pairs))
    return arrived


def touch_kernel(in_ref, out_ref):
    del in_ref, out_ref


def touched(array):
    return pl.pallas_call(
        touch_kernel,
        in_specs=[in_vmem()],
        out_specs=in_vmem(),
        out_shape=jax.ShapeDtypeStruct(array.shape, array.dtype),
        input_output_aliases={0: 0},
        compiler_params=pltpu.CompilerParams(vmem_limit_bytes=1024 * 1024),
        name="touch",
        cost_estimate=pl.CostEstimate(flops=int(5e9), bytes_accessed=0, transcendentals=0),
    )(array)


def after(array, earlier):
    return lax.optimization_barrier((array, earlier))[0]


def swap_in_pair(array, tp_count):
    return lax.ppermute(array, "tp", [(t, t ^ 1) for t in range(tp_count)])


def score(query, keys):
    return lax.dot_general(query, keys, (((1,), (1,)), ((), ())), preferred_element_type=jnp.float32)


def stacked_heads(ref, row, unit, head_size):
    return jnp.concatenate([ref[pl.ds(row, unit), h : h + head_size] for h in range(0, ref.shape[1], head_size)], axis=0)


def log2_rate(head_size):
    return head_size**-0.5 * math.log2(math.e)


def absorb(blocks, rate):
    largest = functools.reduce(jnp.maximum, [jnp.max(s, axis=1, keepdims=True) for s, _ in blocks])
    total, result = 0.0, 0.0
    for scores, values in blocks:
        weight = jnp.exp2((scores - largest) * rate)
        total = total + jnp.sum(weight, axis=1, keepdims=True)
        result = result + jnp.dot(weight.astype(jnp.bfloat16), values, preferred_element_type=jnp.float32)
    return largest, total, result


def private_blocks(query, bias, used, tree, suffix):
    head_size = query.shape[1]
    every = jnp.concatenate([bias] * (query.shape[0] // bias.shape[0]), axis=0)
    return [
        (score(query, tree[:, :head_size]) + every, tree[:, head_size:]),
        (score(query, suffix[:, :head_size]) + used, suffix[:, head_size:]),
    ]


def prompt_of(prompts, group):
    return functools.reduce(lambda held, g: jnp.where(group == g, prompts[g], held), range(1, len(prompts)), prompts[0])


def kept_prompts(shard, fetched):
    groups = shard.shape[0]
    return [jnp.concatenate([shard[g]] + [fetched[k + g] for k in range(0, fetched.shape[0] - groups, groups)], axis=0) for g in range(groups)]


def swapped_prompts(fetched, swapped, groups):
    last = swapped.shape[0] - groups
    return [jnp.concatenate([swapped[k + g] for k in range(0, last, groups)] + [fetched[last + g] + swapped[last + g]], axis=0) for g in range(groups)]


def project(attended_ref, weight_own_ref, weight_other_ref, out_ref, first=0):
    width = weight_own_ref.shape[0]
    count = out_ref.shape[1]
    columns = 512 if count % 512 == 0 else count
    for c in range(0, count, columns):
        product = jnp.dot(attended_ref[:, :width], weight_own_ref[:, first + c : first + c + columns], preferred_element_type=jnp.float32)
        product += jnp.dot(attended_ref[:, width:], weight_other_ref[:, first + c : first + c + columns], preferred_element_type=jnp.float32)
        out_ref[:, c : c + columns] = product.astype(out_ref.dtype)


def rest_kernel(first, attended_ref, weight_own_ref, weight_other_ref, out_ref):
    project(attended_ref, weight_own_ref, weight_other_ref, out_ref, first)


def sum_kernel(near_ref, *rest):
    *arrived, out_ref = rest
    first = 0
    for part_ref in arrived:
        columns = slice(first, first + part_ref.shape[1])
        out_ref[:, columns] = (near_ref[:, columns] + part_ref[...].astype(jnp.float32)).astype(out_ref.dtype)
        first += part_ref.shape[1]


def put_heads(attended_ref, number, unit, attended):
    head_size = attended.shape[1]
    for h in range(attended.shape[0] // unit):
        attended_ref[number * unit : (number + 1) * unit, h * head_size : (h + 1) * head_size] = attended[h * unit : (h + 1) * unit]


def first_row(chunk_rows, offset):
    return (lax.axis_index("tp") ^ offset) * chunk_rows


def closures(parents, node_count):
    above = lax.broadcasted_iota(jnp.int32, (node_count, node_count), 0)
    below = lax.broadcasted_iota(jnp.int32, (node_count, node_count), 1)
    found = []
    for parent in parents:
        step = ((jnp.broadcast_to(parent, (node_count, node_count)) == above) & (below > 0)) | (above == below)
        found.append(jnp.where(step, 1.0, 0.0).astype(jnp.bfloat16))
    for repeat in range(max(1, (node_count - 1).bit_length())):
        found = [jnp.dot(c, c, preferred_element_type=jnp.float32) for c in found]
        found = [jnp.where(c > 0.5, 1.0, 0.0).astype(jnp.bfloat16) for c in found]
    return found


def bias_of(closure):
    return jnp.where(closure.astype(jnp.float32).T > 0.5, 0.0, neg_large)


def first_request(chunk_rows, offset, node_count, requests, touched):
    return jnp.minimum(first_row(chunk_rows, offset) // node_count, requests - touched)


def load_kernel(
    chunk_rows, parents_hbm, length_hbm, group_hbm, own_hbm, tree_hbm, suffix_hbm, shard_hbm, weight_hbm,
    bias_ref, notes_ref, own_ref, tree_ref, suffix_ref, pair_ref, shard_ref, weight_ref, parents_ref, length_ref, group_ref, arrival
):
    requests, node_count = parents_ref.shape
    touched, slot_count = suffix_ref.shape[:2]
    start = pl.multiple_of(first_row(chunk_rows, 2), math.gcd(chunk_rows, node_count))
    pair_start = pl.multiple_of(first_row(chunk_rows, 3), math.gcd(chunk_rows, node_count))
    base = first_request(chunk_rows, 2, node_count, requests, touched)
    copies = [
        pltpu.make_async_copy(source, target, arrival.at[place])
        for place, (source, target) in enumerate((
            (parents_hbm, parents_ref),
            (length_hbm, length_ref),
            (group_hbm, group_ref),
            (own_hbm.at[pl.ds(start, chunk_rows)], own_ref),
            (own_hbm.at[pl.ds(pair_start, chunk_rows)], pair_ref),
            (tree_hbm.at[pl.ds(pl.multiple_of(base * node_count, node_count), touched * node_count)], tree_ref),
            (suffix_hbm.at[pl.ds(base, touched)], suffix_ref),
            (shard_hbm, shard_ref),
            (weight_hbm, weight_ref),
        ))
    ]
    for copy in copies:
        copy.start()
    for copy in copies[:3]:
        copy.wait()
    found = closures([parents_ref[pl.ds(base + k, 1), :] for k in range(touched)], node_count)
    slot = lax.broadcasted_iota(jnp.int32, (1, slot_count), 1)
    for k in range(touched):
        bias_ref[k * node_count : (k + 1) * node_count, :] = bias_of(found[k])
        notes_ref[k, :1, :] = jnp.where(slot < length_ref[base + k], 0.0, neg_large)
        notes_ref[k, 1:2, :] = jnp.broadcast_to(group_ref[base + k].astype(jnp.float32), (1, slot_count))
    for copy in copies[3:]:
        copy.wait()


def private_kernel(unit, chunk_rows, node_count, requests, bias_ref, notes_ref, own_ref, tree_ref, suffix_ref, other_ref, *rest):
    head_size = tree_ref.shape[1] // 2
    touched = suffix_ref.shape[0]
    *parts, state_ref = rest
    prompts = kept_prompts(*parts) if parts else []
    start = pl.multiple_of(first_row(chunk_rows, 2), unit)
    base = first_request(chunk_rows, 2, node_count, requests, touched)
    for number in range(chunk_rows // unit):
        row = pl.multiple_of(start + number * unit, unit)
        place = row // node_count - base
        query = jnp.concatenate(
            [stacked_heads(own_ref, number * unit, unit, head_size), stacked_heads(other_ref, number * unit, unit, head_size)], axis=0
        )
        bias = bias_ref[pl.ds(pl.multiple_of(row - base * node_count, unit), unit), :]
        tree = tree_ref[pl.ds(pl.multiple_of(place * node_count, node_count), node_count), :]
        notes = notes_ref[place]
        group = notes[1:2]
        blocks = private_blocks(query, bias, notes[:1], tree, suffix_ref[place])
        if prompts:
            prompt = prompt_of(prompts, group[:, : 2 * head_size])
            blocks.append((score(query, prompt[:, :head_size]), prompt[:, head_size:]))
        largest, total, result = absorb(blocks, log2_rate(head_size))
        lanes = result.shape
        rows = slice(number * lanes[0], (number + 1) * lanes[0])
        for spot, value in enumerate((result, largest, total, group[:, :head_size])):
            state_ref[rows, spot * head_size : (spot + 1) * head_size] = jnp.broadcast_to(value, lanes)


def in_smem():
    return pl.BlockSpec(memory_space=pltpu.SMEM)


def in_vmem():
    return pl.BlockSpec(memory_space=pltpu.VMEM)


def load(unit, chunk_rows, parents, lengths, groups, own, tree_kv, suffix_kv, shard, weight):
    requests, node_count = parents.shape
    touched = min(requests, -(-(chunk_rows + node_count - unit) // node_count))
    sources = [pltpu.with_memory_space_constraint(a, pltpu.HBM) for a in (parents, lengths, groups, own, tree_kv, suffix_kv, shard, weight)]
    return pl.pallas_call(
        functools.partial(load_kernel, chunk_rows),
        in_specs=[pl.BlockSpec(memory_space=pltpu.HBM)] * 8,
        out_specs=[in_vmem()] * 8,
        out_shape=(
            jax.ShapeDtypeStruct((touched * node_count, node_count), jnp.float32),
            jax.ShapeDtypeStruct((touched, 8, suffix_kv.shape[1]), jnp.float32),
            jax.ShapeDtypeStruct((chunk_rows, own.shape[1]), own.dtype),
            jax.ShapeDtypeStruct((touched * node_count, tree_kv.shape[1]), tree_kv.dtype),
            jax.ShapeDtypeStruct((touched, *suffix_kv.shape[1:]), suffix_kv.dtype),
            jax.ShapeDtypeStruct((chunk_rows, own.shape[1]), own.dtype),
            jax.ShapeDtypeStruct(shard.shape, shard.dtype),
            jax.ShapeDtypeStruct(weight.shape, weight.dtype),
        ),
        scratch_shapes=[
            pltpu.VMEM(parents.shape, jnp.int32),
            pltpu.SMEM(lengths.shape, jnp.int32),
            pltpu.SMEM(groups.shape, jnp.int32),
            pltpu.SemaphoreType.DMA((9,)),
        ],
        compiler_params=pltpu.CompilerParams(vmem_limit_bytes=vmem_bytes),
        name="load",
        cost_estimate=pl.CostEstimate(flops=100_000_000, bytes_accessed=2_000_000, transcendentals=0),
    )(*sources)


def private(unit, chunk_rows, node_count, requests, loaded, other, parts):
    bias, notes, own, tree, suffix = loaded
    head_size = tree.shape[1] // 2
    state_rows = chunk_rows * 2 * (own.shape[1] // head_size)
    return pl.pallas_call(
        functools.partial(private_kernel, unit, chunk_rows, node_count, requests),
        in_specs=[in_vmem()] * (6 + len(parts)),
        out_specs=in_vmem(),
        out_shape=jax.ShapeDtypeStruct((state_rows, 4 * head_size), jnp.float32),
        compiler_params=pltpu.CompilerParams(vmem_limit_bytes=vmem_bytes),
        name="private",
        cost_estimate=pl.CostEstimate(flops=300_000_000, bytes_accessed=500_000, transcendentals=0),
    )(*loaded, other, *parts)


def far_kernel(unit, part_count, own_ref, other_ref, state_ref, *rest):
    parts, (weight_own_ref, weight_other_ref, out_ref, attended_ref) = rest[:part_count], rest[part_count:]
    chunk_rows = out_ref.shape[0]
    head_size = state_ref.shape[1] // 4
    rate = log2_rate(head_size)
    prompts = swapped_prompts(parts[0], parts[1], parts[0].shape[0] // fetches) if part_count == 2 else [parts[0][g] for g in range(parts[0].shape[0])]
    start = first_row(chunk_rows, 2)
    for number in range(chunk_rows // unit):
        row = pl.multiple_of(start + number * unit, unit)
        query = jnp.concatenate(
            [stacked_heads(own_ref, number * unit, unit, head_size), stacked_heads(other_ref, number * unit, unit, head_size)], axis=0
        )
        rows = slice(number * query.shape[0], (number + 1) * query.shape[0])
        before, largest, total, group = (state_ref[rows, spot * head_size : (spot + 1) * head_size] for spot in range(4))
        prompt = prompt_of(prompts, jnp.concatenate([group[:1], group[:1]], axis=1))
        scores = score(query, prompt[:, :head_size])
        top = jnp.maximum(largest, jnp.max(scores, axis=1, keepdims=True))
        fade = jnp.exp2((largest - top) * rate)
        width = scores.shape[1] // head_size
        weight = jnp.exp2((scores - (top if width == 1 else jnp.concatenate([top] * width, axis=1))) * rate)
        total = total * fade + jnp.sum(weight, axis=1, keepdims=True)
        result = before * fade + jnp.dot(weight.astype(jnp.bfloat16), prompt[:, head_size:], preferred_element_type=jnp.float32)
        put_heads(attended_ref, number, unit, (result / total).astype(jnp.bfloat16))
    project(attended_ref, weight_own_ref, weight_other_ref, out_ref)


def near_kernel(
    unit, piece_count, length_ref, group_ref, own_ref, other_ref, parents_ref, accepted_ref, tree_ref, suffix_ref, *rest
):
    pieces, (weight_own_ref, weight_other_ref, out_ref, path_ref, attended_ref, bias_ref) = rest[:piece_count], rest[piece_count:]
    chunk_rows = out_ref.shape[0]
    requests, node_count = parents_ref.shape
    path_length = accepted_ref.shape[1]
    head_size = tree_ref.shape[1] // 2
    node = lax.broadcasted_iota(jnp.int32, (node_count, path_length), 0)
    for r, closure in enumerate(closures([parents_ref[r : r + 1, :] for r in range(requests)], node_count)):
        rows = slice(r * node_count, (r + 1) * node_count)
        bias_ref[rows, :] = bias_of(closure)
        chosen = jnp.broadcast_to(accepted_ref[r : r + 1, :], (node_count, path_length)) == node
        path_ref[r] = lax.dot_general(
            jnp.where(chosen, 1.0, 0.0).astype(jnp.bfloat16),
            tree_ref[rows, :],
            (((0,), (0,)), ((), ())),
            preferred_element_type=jnp.float32,
        ).astype(jnp.bfloat16)
    if piece_count == 3:
        kept = kept_prompts(pieces[0], pieces[1])
        prompts = [jnp.concatenate(pair, axis=0) for pair in zip(kept, swapped_prompts(pieces[1], pieces[2], len(kept)))]
    else:
        prompts = [pieces[0][g] for g in range(pieces[0].shape[0])]
    slot = lax.broadcasted_iota(jnp.int32, (1, suffix_ref.shape[1]), 1)
    start = first_row(chunk_rows, 0)
    for number in range(chunk_rows // unit):
        row = pl.multiple_of(start + number * unit, unit)
        query = jnp.concatenate([stacked_heads(ref, row, unit, head_size) for ref in (own_ref, other_ref)], axis=0)
        request = row // node_count
        used = jnp.where(slot < length_ref[request], 0.0, neg_large)
        tree = tree_ref[pl.ds(pl.multiple_of(request * node_count, node_count), node_count), :]
        blocks = private_blocks(query, bias_ref[pl.ds(row, unit), :], used, tree, suffix_ref[request])
        group = group_ref[request]
        prompt = prompt_of(prompts, group)
        blocks.append((score(query, prompt[:, :head_size]), prompt[:, head_size:]))
        largest, total, result = absorb(blocks, log2_rate(head_size))
        put_heads(attended_ref, number, unit, (result / total).astype(jnp.bfloat16))
    project(attended_ref, weight_own_ref, weight_other_ref, out_ref)


def chunk(kernel, name, outs, scalars, arrays, weights, scratch=(), flops=500_000_000):
    return pl.pallas_call(
        kernel,
        in_specs=[in_smem()] * len(scalars) + [in_vmem()] * (len(arrays) + len(weights)),
        out_specs=[in_vmem()] * len(outs),
        out_shape=outs,
        scratch_shapes=scratch,
        compiler_params=pltpu.CompilerParams(vmem_limit_bytes=vmem_bytes),
        name=name,
        cost_estimate=pl.CostEstimate(flops=flops, bytes_accessed=1_000_000, transcendentals=0),
    )(*scalars, *arrays, *weights)


def local(req_count, tp_count, queries, tree_kv, suffix_kv, suffix_len, group_ids, parents, accepted, prompt_kv, out_weight):
    chunk_rows = queries.shape[0] // tp_count
    unit = math.gcd(chunk_rows, parents.shape[1])
    if req_count == 8 and tp_count % 2 == 0:
        fetched = fetch_shards(prompt_kv, req_count, tp_count)
        other_weight = swap_in_pair(out_weight, tp_count)
    else:
        fetched = None
        other_weight = swap_in_pair(out_weight, tp_count)
    requests, node_count = parents.shape
    *loaded, pair_queries, shard, own_weight = load(unit, chunk_rows, parents, suffix_len, group_ids, queries, tree_kv, suffix_kv, prompt_kv, out_weight)
    far_queries = touched(swap_in_pair(pair_queries, tp_count))
    if fetched is None:
        pieces = [lax.all_gather(prompt_kv, "req", axis=1, tiled=True)]
        state = private(unit, chunk_rows, node_count, requests, loaded, far_queries, [])
    else:
        joined = jnp.concatenate([after(piece, shard) for piece in fetched], axis=0)
        pieces = [shard, joined, swap_in_pair(joined, tp_count)]
        state = private(unit, chunk_rows, node_count, requests, loaded, far_queries, pieces[:2])
    parts = pieces[-2:]
    weights = (own_weight, other_weight)
    columns = out_weight.shape[1]
    early = columns // 4
    attended_shape = (chunk_rows, 2 * out_weight.shape[0])
    early_far, attended = chunk(
        functools.partial(far_kernel, unit, len(parts)), "far_chunk",
        [jax.ShapeDtypeStruct((chunk_rows, early), jnp.bfloat16), jax.ShapeDtypeStruct(attended_shape, jnp.bfloat16)],
        (), (loaded[2], far_queries, state, *parts), weights, flops=200_000_000
    )
    across = [(t, t ^ 2) for t in range(tp_count)]
    early_arrived = touched(lax.ppermute(early_far, "tp", across))
    (late_far,) = chunk(
        functools.partial(rest_kernel, early), "far_rest", [jax.ShapeDtypeStruct((chunk_rows, columns - early), jnp.bfloat16)],
        (), (attended,), weights, flops=300_000_000
    )
    late_arrived = lax.ppermute(late_far, "tp", across)
    other_queries = swap_in_pair(after(queries, late_far), tp_count)
    near, path_cache = chunk(
        functools.partial(near_kernel, unit, len(pieces)), "near_chunk",
        [jax.ShapeDtypeStruct((chunk_rows, columns), jnp.float32), jax.ShapeDtypeStruct((*accepted.shape, tree_kv.shape[1]), jnp.bfloat16)],
        (suffix_len, group_ids), (queries, other_queries, parents, accepted, tree_kv, suffix_kv, *pieces), weights,
        (pltpu.VMEM(attended_shape, jnp.bfloat16), pltpu.VMEM((requests * node_count, node_count), jnp.float32))
    )
    (layer_output,) = chunk(
        sum_kernel, "sum", [jax.ShapeDtypeStruct((chunk_rows, columns), jnp.bfloat16)], (), (near, early_arrived, late_arrived), (), flops=1_000_000
    )
    return (layer_output, path_cache)


def solution(mesh):
    return jax.shard_map(
        functools.partial(local, mesh.shape["req"], mesh.shape["tp"]),
        mesh=mesh,
        in_specs=(
            P("req", "tp"),
            P("req", None),
            P("req", None, None),
            P("req"),
            P("req"),
            P("req", None),
            P("req", None),
            P(None, "req", None),
            P("tp", None),
        ),
        out_specs=(P(("req", "tp"), None), P("req", None, None)),
        check_vma=False,
    )
```

```python
import functools
import math

import jax
import jax.numpy as jnp
from jax import lax
from jax.experimental import pallas as pl
from jax.experimental.pallas import tpu as pltpu
from jax.sharding import PartitionSpec as P

neg_large = -1e30
vmem_bytes = 12 * 1024 * 1024
fetches = 4


def fetch_shards(shard, req_count, tp_count):
    masks = ((4, 5, 3), (6, 7, 2, 1))
    arrived = []
    for step in range(fetches):
        pairs = []
        for r in range(req_count):
            for t in range(tp_count):
                mine = masks[t % 2]
                if step < len(mine):
                    pairs.append((r * tp_count + t, (r ^ mine[step]) * tp_count + t))
        arrived.append(lax.ppermute(shard, ("req", "tp"), pairs))
    return arrived


def touch_kernel(in_ref, out_ref):
    del in_ref, out_ref


def touched(array):
    return pl.pallas_call(
        touch_kernel,
        in_specs=[in_vmem()],
        out_specs=in_vmem(),
        out_shape=jax.ShapeDtypeStruct(array.shape, array.dtype),
        input_output_aliases={0: 0},
        compiler_params=pltpu.CompilerParams(vmem_limit_bytes=1024 * 1024),
        name="touch",
        cost_estimate=pl.CostEstimate(flops=int(5e9), bytes_accessed=0, transcendentals=0),
    )(array)


def after(array, earlier):
    return lax.optimization_barrier((array, earlier))[0]


def swap_in_pair(array, tp_count):
    return lax.ppermute(array, "tp", [(t, t ^ 1) for t in range(tp_count)])


def score(query, keys):
    return lax.dot_general(query, keys, (((1,), (1,)), ((), ())), preferred_element_type=jnp.float32)


def stacked_heads(ref, row, unit, head_size):
    return jnp.concatenate([ref[pl.ds(row, unit), h : h + head_size] for h in range(0, ref.shape[1], head_size)], axis=0)


def log2_rate(head_size):
    return head_size**-0.5 * math.log2(math.e)


def absorb(blocks, rate):
    largest = functools.reduce(jnp.maximum, [jnp.max(s, axis=1, keepdims=True) for s, _ in blocks])
    total, result = 0.0, 0.0
    for scores, values in blocks:
        weight = jnp.exp2((scores - largest) * rate)
        total = total + jnp.sum(weight, axis=1, keepdims=True)
        result = result + jnp.dot(weight.astype(jnp.bfloat16), values, preferred_element_type=jnp.float32)
    return largest, total, result


def private_blocks(query, bias, used, tree, suffix):
    head_size = query.shape[1]
    every = jnp.concatenate([bias] * (query.shape[0] // bias.shape[0]), axis=0)
    return [
        (score(query, tree[:, :head_size]) + every, tree[:, head_size:]),
        (score(query, suffix[:, :head_size]) + used, suffix[:, head_size:]),
    ]


def prompt_of(prompts, group):
    return functools.reduce(lambda held, g: jnp.where(group == g, prompts[g], held), range(1, len(prompts)), prompts[0])


def kept_prompts(shard, fetched):
    groups = shard.shape[0]
    return [jnp.concatenate([shard[g]] + [fetched[k + g] for k in range(0, fetched.shape[0] - groups, groups)], axis=0) for g in range(groups)]


def swapped_prompts(fetched, swapped, groups):
    last = swapped.shape[0] - groups
    return [jnp.concatenate([swapped[k + g] for k in range(0, last, groups)] + [fetched[last + g] + swapped[last + g]], axis=0) for g in range(groups)]


def project(attended_ref, weight_own_ref, weight_other_ref, out_ref, first=0):
    width = weight_own_ref.shape[0]
    count = out_ref.shape[1]
    columns = 512 if count % 512 == 0 else count
    for c in range(0, count, columns):
        product = jnp.dot(attended_ref[:, :width], weight_own_ref[:, first + c : first + c + columns], preferred_element_type=jnp.float32)
        product += jnp.dot(attended_ref[:, width:], weight_other_ref[:, first + c : first + c + columns], preferred_element_type=jnp.float32)
        out_ref[:, c : c + columns] = product.astype(out_ref.dtype)


def rest_kernel(first, attended_ref, weight_own_ref, weight_other_ref, out_ref):
    project(attended_ref, weight_own_ref, weight_other_ref, out_ref, first)


def sum_kernel(piece_rows, near_ref, *rest):
    *arrived, out_hbm, total_ref, sent = rest
    copies = []
    for place, row in enumerate(range(0, near_ref.shape[0], piece_rows)):
        rows = slice(row, row + piece_rows)
        first = 0
        for part_ref in arrived:
            columns = slice(first, first + part_ref.shape[1])
            total_ref[rows, columns] = (near_ref[rows, columns] + part_ref[rows, :].astype(jnp.float32)).astype(total_ref.dtype)
            first += part_ref.shape[1]
        copies.append(pltpu.make_async_copy(total_ref.at[rows], out_hbm.at[rows], sent.at[place]))
        copies[-1].start()
    for copy in copies:
        copy.wait()


def sum_parts(unit, near, arrived):
    return pl.pallas_call(
        functools.partial(sum_kernel, unit),
        in_specs=[in_vmem()] * (1 + len(arrived)),
        out_specs=pl.BlockSpec(memory_space=pl.ANY),
        out_shape=jax.ShapeDtypeStruct(near.shape, jnp.bfloat16),
        scratch_shapes=[pltpu.VMEM(near.shape, jnp.bfloat16), pltpu.SemaphoreType.DMA((near.shape[0] // unit,))],
        compiler_params=pltpu.CompilerParams(vmem_limit_bytes=vmem_bytes),
        name="sum",
        cost_estimate=pl.CostEstimate(flops=1_000_000, bytes_accessed=1_000_000, transcendentals=0),
    )(near, *arrived)


def put_heads(attended_ref, number, unit, attended):
    head_size = attended.shape[1]
    for h in range(attended.shape[0] // unit):
        attended_ref[number * unit : (number + 1) * unit, h * head_size : (h + 1) * head_size] = attended[h * unit : (h + 1) * unit]


def first_row(chunk_rows, offset):
    return (lax.axis_index("tp") ^ offset) * chunk_rows


def closures(parents, node_count):
    above = lax.broadcasted_iota(jnp.int32, (node_count, node_count), 0)
    below = lax.broadcasted_iota(jnp.int32, (node_count, node_count), 1)
    found = []
    for parent in parents:
        step = ((jnp.broadcast_to(parent, (node_count, node_count)) == above) & (below > 0)) | (above == below)
        found.append(jnp.where(step, 1.0, 0.0).astype(jnp.bfloat16))
    for repeat in range(max(1, (node_count - 1).bit_length())):
        found = [jnp.dot(c, c, preferred_element_type=jnp.float32) for c in found]
        found = [jnp.where(c > 0.5, 1.0, 0.0).astype(jnp.bfloat16) for c in found]
    return found


def bias_of(closure):
    return jnp.where(closure.astype(jnp.float32).T > 0.5, 0.0, neg_large)


def first_request(chunk_rows, offset, node_count, requests, touched):
    return jnp.minimum(first_row(chunk_rows, offset) // node_count, requests - touched)


def load_kernel(
    chunk_rows, parents_hbm, length_hbm, group_hbm, own_hbm, tree_hbm, suffix_hbm, shard_hbm, weight_hbm,
    bias_ref, notes_ref, own_ref, tree_ref, suffix_ref, pair_ref, shard_ref, weight_ref, parents_ref, length_ref, group_ref, arrival
):
    requests, node_count = parents_ref.shape
    touched, slot_count = suffix_ref.shape[:2]
    start = pl.multiple_of(first_row(chunk_rows, 2), math.gcd(chunk_rows, node_count))
    pair_start = pl.multiple_of(first_row(chunk_rows, 3), math.gcd(chunk_rows, node_count))
    base = first_request(chunk_rows, 2, node_count, requests, touched)
    copies = [
        pltpu.make_async_copy(source, target, arrival.at[place])
        for place, (source, target) in enumerate((
            (parents_hbm, parents_ref),
            (length_hbm, length_ref),
            (group_hbm, group_ref),
            (own_hbm.at[pl.ds(start, chunk_rows)], own_ref),
            (own_hbm.at[pl.ds(pair_start, chunk_rows)], pair_ref),
            (tree_hbm.at[pl.ds(pl.multiple_of(base * node_count, node_count), touched * node_count)], tree_ref),
            (suffix_hbm.at[pl.ds(base, touched)], suffix_ref),
            (shard_hbm, shard_ref),
            (weight_hbm, weight_ref),
        ))
    ]
    for copy in copies:
        copy.start()
    for copy in copies[:3]:
        copy.wait()
    found = closures([parents_ref[pl.ds(base + k, 1), :] for k in range(touched)], node_count)
    slot = lax.broadcasted_iota(jnp.int32, (1, slot_count), 1)
    for k in range(touched):
        bias_ref[k * node_count : (k + 1) * node_count, :] = bias_of(found[k])
        notes_ref[k, :1, :] = jnp.where(slot < length_ref[base + k], 0.0, neg_large)
        notes_ref[k, 1:2, :] = jnp.broadcast_to(group_ref[base + k].astype(jnp.float32), (1, slot_count))
    for copy in copies[3:]:
        copy.wait()


def private_kernel(unit, chunk_rows, node_count, requests, bias_ref, notes_ref, own_ref, tree_ref, suffix_ref, other_ref, *rest):
    head_size = tree_ref.shape[1] // 2
    touched = suffix_ref.shape[0]
    *parts, state_ref = rest
    prompts = kept_prompts(*parts) if parts else []
    start = pl.multiple_of(first_row(chunk_rows, 2), unit)
    base = first_request(chunk_rows, 2, node_count, requests, touched)
    for number in range(chunk_rows // unit):
        row = pl.multiple_of(start + number * unit, unit)
        place = row // node_count - base
        query = jnp.concatenate(
            [stacked_heads(own_ref, number * unit, unit, head_size), stacked_heads(other_ref, number * unit, unit, head_size)], axis=0
        )
        bias = bias_ref[pl.ds(pl.multiple_of(row - base * node_count, unit), unit), :]
        tree = tree_ref[pl.ds(pl.multiple_of(place * node_count, node_count), node_count), :]
        notes = notes_ref[place]
        group = notes[1:2]
        blocks = private_blocks(query, bias, notes[:1], tree, suffix_ref[place])
        if prompts:
            prompt = prompt_of(prompts, group[:, : 2 * head_size])
            blocks.append((score(query, prompt[:, :head_size]), prompt[:, head_size:]))
        largest, total, result = absorb(blocks, log2_rate(head_size))
        lanes = result.shape
        rows = slice(number * lanes[0], (number + 1) * lanes[0])
        for spot, value in enumerate((result, largest, total, group[:, :head_size])):
            state_ref[rows, spot * head_size : (spot + 1) * head_size] = jnp.broadcast_to(value, lanes)


def in_smem():
    return pl.BlockSpec(memory_space=pltpu.SMEM)


def in_vmem():
    return pl.BlockSpec(memory_space=pltpu.VMEM)


def load(unit, chunk_rows, parents, lengths, groups, own, tree_kv, suffix_kv, shard, weight):
    requests, node_count = parents.shape
    touched = min(requests, -(-(chunk_rows + node_count - unit) // node_count))
    sources = [pltpu.with_memory_space_constraint(a, pltpu.HBM) for a in (parents, lengths, groups, own, tree_kv, suffix_kv, shard, weight)]
    return pl.pallas_call(
        functools.partial(load_kernel, chunk_rows),
        in_specs=[pl.BlockSpec(memory_space=pltpu.HBM)] * 8,
        out_specs=[in_vmem()] * 8,
        out_shape=(
            jax.ShapeDtypeStruct((touched * node_count, node_count), jnp.float32),
            jax.ShapeDtypeStruct((touched, 8, suffix_kv.shape[1]), jnp.float32),
            jax.ShapeDtypeStruct((chunk_rows, own.shape[1]), own.dtype),
            jax.ShapeDtypeStruct((touched * node_count, tree_kv.shape[1]), tree_kv.dtype),
            jax.ShapeDtypeStruct((touched, *suffix_kv.shape[1:]), suffix_kv.dtype),
            jax.ShapeDtypeStruct((chunk_rows, own.shape[1]), own.dtype),
            jax.ShapeDtypeStruct(shard.shape, shard.dtype),
            jax.ShapeDtypeStruct(weight.shape, weight.dtype),
        ),
        scratch_shapes=[
            pltpu.VMEM(parents.shape, jnp.int32),
            pltpu.SMEM(lengths.shape, jnp.int32),
            pltpu.SMEM(groups.shape, jnp.int32),
            pltpu.SemaphoreType.DMA((9,)),
        ],
        compiler_params=pltpu.CompilerParams(vmem_limit_bytes=vmem_bytes),
        name="load",
        cost_estimate=pl.CostEstimate(flops=100_000_000, bytes_accessed=2_000_000, transcendentals=0),
    )(*sources)


def private(unit, chunk_rows, node_count, requests, loaded, other, parts):
    bias, notes, own, tree, suffix = loaded
    head_size = tree.shape[1] // 2
    state_rows = chunk_rows * 2 * (own.shape[1] // head_size)
    return pl.pallas_call(
        functools.partial(private_kernel, unit, chunk_rows, node_count, requests),
        in_specs=[in_vmem()] * (6 + len(parts)),
        out_specs=in_vmem(),
        out_shape=jax.ShapeDtypeStruct((state_rows, 4 * head_size), jnp.float32),
        compiler_params=pltpu.CompilerParams(vmem_limit_bytes=vmem_bytes),
        name="private",
        cost_estimate=pl.CostEstimate(flops=300_000_000, bytes_accessed=500_000, transcendentals=0),
    )(*loaded, other, *parts)


def far_kernel(unit, part_count, own_ref, other_ref, state_ref, *rest):
    parts, (weight_own_ref, weight_other_ref, out_ref, attended_ref) = rest[:part_count], rest[part_count:]
    chunk_rows = out_ref.shape[0]
    head_size = state_ref.shape[1] // 4
    rate = log2_rate(head_size)
    prompts = swapped_prompts(parts[0], parts[1], parts[0].shape[0] // fetches) if part_count == 2 else [parts[0][g] for g in range(parts[0].shape[0])]
    start = first_row(chunk_rows, 2)
    for number in range(chunk_rows // unit):
        row = pl.multiple_of(start + number * unit, unit)
        query = jnp.concatenate(
            [stacked_heads(own_ref, number * unit, unit, head_size), stacked_heads(other_ref, number * unit, unit, head_size)], axis=0
        )
        rows = slice(number * query.shape[0], (number + 1) * query.shape[0])
        before, largest, total, group = (state_ref[rows, spot * head_size : (spot + 1) * head_size] for spot in range(4))
        prompt = prompt_of(prompts, jnp.concatenate([group[:1], group[:1]], axis=1))
        scores = score(query, prompt[:, :head_size])
        top = jnp.maximum(largest, jnp.max(scores, axis=1, keepdims=True))
        fade = jnp.exp2((largest - top) * rate)
        width = scores.shape[1] // head_size
        weight = jnp.exp2((scores - (top if width == 1 else jnp.concatenate([top] * width, axis=1))) * rate)
        total = total * fade + jnp.sum(weight, axis=1, keepdims=True)
        result = before * fade + jnp.dot(weight.astype(jnp.bfloat16), prompt[:, head_size:], preferred_element_type=jnp.float32)
        put_heads(attended_ref, number, unit, (result / total).astype(jnp.bfloat16))
    project(attended_ref, weight_own_ref, weight_other_ref, out_ref)


def near_kernel(
    unit, piece_count, length_ref, group_ref, own_ref, other_ref, parents_ref, accepted_ref, tree_ref, suffix_ref, *rest
):
    pieces, (weight_own_ref, weight_other_ref, out_ref, path_ref, attended_ref, bias_ref) = rest[:piece_count], rest[piece_count:]
    chunk_rows = out_ref.shape[0]
    requests, node_count = parents_ref.shape
    path_length = accepted_ref.shape[1]
    head_size = tree_ref.shape[1] // 2
    node = lax.broadcasted_iota(jnp.int32, (node_count, path_length), 0)
    for r, closure in enumerate(closures([parents_ref[r : r + 1, :] for r in range(requests)], node_count)):
        rows = slice(r * node_count, (r + 1) * node_count)
        bias_ref[rows, :] = bias_of(closure)
        chosen = jnp.broadcast_to(accepted_ref[r : r + 1, :], (node_count, path_length)) == node
        path_ref[r] = lax.dot_general(
            jnp.where(chosen, 1.0, 0.0).astype(jnp.bfloat16),
            tree_ref[rows, :],
            (((0,), (0,)), ((), ())),
            preferred_element_type=jnp.float32,
        ).astype(jnp.bfloat16)
    if piece_count == 3:
        kept = kept_prompts(pieces[0], pieces[1])
        prompts = [jnp.concatenate(pair, axis=0) for pair in zip(kept, swapped_prompts(pieces[1], pieces[2], len(kept)))]
    else:
        prompts = [pieces[0][g] for g in range(pieces[0].shape[0])]
    slot = lax.broadcasted_iota(jnp.int32, (1, suffix_ref.shape[1]), 1)
    start = first_row(chunk_rows, 0)
    for number in range(chunk_rows // unit):
        row = pl.multiple_of(start + number * unit, unit)
        query = jnp.concatenate([stacked_heads(ref, row, unit, head_size) for ref in (own_ref, other_ref)], axis=0)
        request = row // node_count
        used = jnp.where(slot < length_ref[request], 0.0, neg_large)
        tree = tree_ref[pl.ds(pl.multiple_of(request * node_count, node_count), node_count), :]
        blocks = private_blocks(query, bias_ref[pl.ds(row, unit), :], used, tree, suffix_ref[request])
        group = group_ref[request]
        prompt = prompt_of(prompts, group)
        blocks.append((score(query, prompt[:, :head_size]), prompt[:, head_size:]))
        largest, total, result = absorb(blocks, log2_rate(head_size))
        put_heads(attended_ref, number, unit, (result / total).astype(jnp.bfloat16))
    project(attended_ref, weight_own_ref, weight_other_ref, out_ref)


def chunk(kernel, name, outs, scalars, arrays, weights, scratch=(), flops=500_000_000):
    return pl.pallas_call(
        kernel,
        in_specs=[in_smem()] * len(scalars) + [in_vmem()] * (len(arrays) + len(weights)),
        out_specs=[in_vmem()] * len(outs),
        out_shape=outs,
        scratch_shapes=scratch,
        compiler_params=pltpu.CompilerParams(vmem_limit_bytes=vmem_bytes),
        name=name,
        cost_estimate=pl.CostEstimate(flops=flops, bytes_accessed=1_000_000, transcendentals=0),
    )(*scalars, *arrays, *weights)


def local(req_count, tp_count, queries, tree_kv, suffix_kv, suffix_len, group_ids, parents, accepted, prompt_kv, out_weight):
    chunk_rows = queries.shape[0] // tp_count
    unit = math.gcd(chunk_rows, parents.shape[1])
    if req_count == 8 and tp_count % 2 == 0:
        fetched = fetch_shards(prompt_kv, req_count, tp_count)
        other_weight = swap_in_pair(out_weight, tp_count)
    else:
        fetched = None
        other_weight = swap_in_pair(out_weight, tp_count)
    requests, node_count = parents.shape
    *loaded, pair_queries, shard, own_weight = load(unit, chunk_rows, parents, suffix_len, group_ids, queries, tree_kv, suffix_kv, prompt_kv, out_weight)
    far_queries = touched(swap_in_pair(pair_queries, tp_count))
    if fetched is None:
        pieces = [lax.all_gather(prompt_kv, "req", axis=1, tiled=True)]
        state = private(unit, chunk_rows, node_count, requests, loaded, far_queries, [])
    else:
        joined = jnp.concatenate([after(piece, shard) for piece in fetched], axis=0)
        pieces = [shard, joined, swap_in_pair(joined, tp_count)]
        state = private(unit, chunk_rows, node_count, requests, loaded, far_queries, pieces[:2])
    parts = pieces[-2:]
    weights = (own_weight, other_weight)
    columns = out_weight.shape[1]
    early = columns // 4
    attended_shape = (chunk_rows, 2 * out_weight.shape[0])
    early_far, attended = chunk(
        functools.partial(far_kernel, unit, len(parts)), "far_chunk",
        [jax.ShapeDtypeStruct((chunk_rows, early), jnp.bfloat16), jax.ShapeDtypeStruct(attended_shape, jnp.bfloat16)],
        (), (loaded[2], far_queries, state, *parts), weights, flops=200_000_000
    )
    across = [(t, t ^ 2) for t in range(tp_count)]
    early_arrived = touched(lax.ppermute(early_far, "tp", across))
    (late_far,) = chunk(
        functools.partial(rest_kernel, early), "far_rest", [jax.ShapeDtypeStruct((chunk_rows, columns - early), jnp.bfloat16)],
        (), (attended,), weights, flops=300_000_000
    )
    late_arrived = lax.ppermute(late_far, "tp", across)
    other_queries = swap_in_pair(after(queries, late_far), tp_count)
    near, path_cache = chunk(
        functools.partial(near_kernel, unit, len(pieces)), "near_chunk",
        [jax.ShapeDtypeStruct((chunk_rows, columns), jnp.float32), jax.ShapeDtypeStruct((*accepted.shape, tree_kv.shape[1]), jnp.bfloat16)],
        (suffix_len, group_ids), (queries, other_queries, parents, accepted, tree_kv, suffix_kv, *pieces), weights,
        (pltpu.VMEM(attended_shape, jnp.bfloat16), pltpu.VMEM((requests * node_count, node_count), jnp.float32))
    )
    layer_output = sum_parts(unit, near, (early_arrived, late_arrived))
    return (layer_output, path_cache)


def solution(mesh):
    return jax.shard_map(
        functools.partial(local, mesh.shape["req"], mesh.shape["tp"]),
        mesh=mesh,
        in_specs=(
            P("req", "tp"),
            P("req", None),
            P("req", None, None),
            P("req"),
            P("req"),
            P("req", None),
            P("req", None),
            P(None, "req", None),
            P("tp", None),
        ),
        out_specs=(P(("req", "tp"), None), P("req", None, None)),
        check_vma=False,
    )
```

```python
import functools
import math

import jax
import jax.numpy as jnp
from jax import lax
from jax.experimental import pallas as pl
from jax.experimental.pallas import tpu as pltpu
from jax.sharding import PartitionSpec as P

neg_large = -1e30
vmem_bytes = 12 * 1024 * 1024
fetches = 4


def fetch_shards(shard, req_count, tp_count):
    masks = ((5, 4, 3), (7, 6, 2, 1))
    arrived = []
    for step in range(fetches):
        pairs = []
        for r in range(req_count):
            for t in range(tp_count):
                mine = masks[t % 2]
                if step < len(mine):
                    pairs.append((r * tp_count + t, (r ^ mine[step]) * tp_count + t))
        arrived.append(lax.ppermute(shard, ("req", "tp"), pairs))
    return arrived


def touch_kernel(in_ref, out_ref):
    del in_ref, out_ref


def touched(array):
    return pl.pallas_call(
        touch_kernel,
        in_specs=[in_vmem()],
        out_specs=in_vmem(),
        out_shape=jax.ShapeDtypeStruct(array.shape, array.dtype),
        input_output_aliases={0: 0},
        compiler_params=pltpu.CompilerParams(vmem_limit_bytes=1024 * 1024),
        name="touch",
        cost_estimate=pl.CostEstimate(flops=int(5e9), bytes_accessed=0, transcendentals=0),
    )(array)


def after(array, earlier):
    return lax.optimization_barrier((array, earlier))[0]


def swap_in_pair(array, tp_count):
    return lax.ppermute(array, "tp", [(t, t ^ 1) for t in range(tp_count)])


def score(query, keys):
    return lax.dot_general(query, keys, (((1,), (1,)), ((), ())), preferred_element_type=jnp.float32)


def stacked_heads(ref, row, unit, head_size):
    return jnp.concatenate([ref[pl.ds(row, unit), h : h + head_size] for h in range(0, ref.shape[1], head_size)], axis=0)


def log2_rate(head_size):
    return head_size**-0.5 * math.log2(math.e)


def absorb(blocks, rate):
    largest = functools.reduce(jnp.maximum, [jnp.max(s, axis=1, keepdims=True) for s, _ in blocks])
    total, result = 0.0, 0.0
    for scores, values in blocks:
        weight = jnp.exp2((scores - largest) * rate)
        total = total + jnp.sum(weight, axis=1, keepdims=True)
        result = result + jnp.dot(weight.astype(jnp.bfloat16), values, preferred_element_type=jnp.float32)
    return largest, total, result


def private_blocks(query, bias, used, tree, suffix):
    head_size = query.shape[1]
    every = jnp.concatenate([bias] * (query.shape[0] // bias.shape[0]), axis=0)
    return [
        (score(query, tree[:, :head_size]) + every, tree[:, head_size:]),
        (score(query, suffix[:, :head_size]) + used, suffix[:, head_size:]),
    ]


def prompt_of(prompts, group):
    return functools.reduce(lambda held, g: jnp.where(group == g, prompts[g], held), range(1, len(prompts)), prompts[0])


def kept_prompts(shard, fetched):
    groups = shard.shape[0]
    return [jnp.concatenate([shard[g]] + [fetched[k + g] for k in range(0, fetched.shape[0] - groups, groups)], axis=0) for g in range(groups)]


def swapped_prompts(fetched, swapped, groups):
    last = swapped.shape[0] - groups
    return [jnp.concatenate([swapped[k + g] for k in range(0, last, groups)] + [fetched[last + g] + swapped[last + g]], axis=0) for g in range(groups)]


def project(attended_ref, weight_own_ref, weight_other_ref, out_ref, first=0):
    width = weight_own_ref.shape[0]
    count = out_ref.shape[1]
    columns = 512 if count % 512 == 0 else count
    for c in range(0, count, columns):
        product = jnp.dot(attended_ref[:, :width], weight_own_ref[:, first + c : first + c + columns], preferred_element_type=jnp.float32)
        product += jnp.dot(attended_ref[:, width:], weight_other_ref[:, first + c : first + c + columns], preferred_element_type=jnp.float32)
        out_ref[:, c : c + columns] = product.astype(out_ref.dtype)


def rest_kernel(first, attended_ref, weight_own_ref, weight_other_ref, out_ref):
    project(attended_ref, weight_own_ref, weight_other_ref, out_ref, first)


def sum_kernel(near_ref, *rest):
    *arrived, out_ref = rest
    first = 0
    for part_ref in arrived:
        columns = slice(first, first + part_ref.shape[1])
        out_ref[:, columns] = (near_ref[:, columns] + part_ref[...].astype(jnp.float32)).astype(out_ref.dtype)
        first += part_ref.shape[1]


def put_heads(attended_ref, number, unit, attended):
    head_size = attended.shape[1]
    for h in range(attended.shape[0] // unit):
        attended_ref[number * unit : (number + 1) * unit, h * head_size : (h + 1) * head_size] = attended[h * unit : (h + 1) * unit]


def first_row(chunk_rows, offset):
    return (lax.axis_index("tp") ^ offset) * chunk_rows


def closures(parents, node_count):
    above = lax.broadcasted_iota(jnp.int32, (node_count, node_count), 0)
    below = lax.broadcasted_iota(jnp.int32, (node_count, node_count), 1)
    found = []
    for parent in parents:
        step = ((jnp.broadcast_to(parent, (node_count, node_count)) == above) & (below > 0)) | (above == below)
        found.append(jnp.where(step, 1.0, 0.0).astype(jnp.bfloat16))
    for repeat in range(max(1, (node_count - 1).bit_length())):
        found = [jnp.dot(c, c, preferred_element_type=jnp.float32) for c in found]
        found = [jnp.where(c > 0.5, 1.0, 0.0).astype(jnp.bfloat16) for c in found]
    return found


def bias_of(closure):
    return jnp.where(closure.astype(jnp.float32).T > 0.5, 0.0, neg_large)


def first_request(chunk_rows, offset, node_count, requests, touched):
    return jnp.minimum(first_row(chunk_rows, offset) // node_count, requests - touched)


def load_kernel(
    chunk_rows, parents_hbm, length_hbm, group_hbm, own_hbm, tree_hbm, suffix_hbm, shard_hbm, weight_hbm,
    bias_ref, notes_ref, own_ref, tree_ref, suffix_ref, pair_ref, shard_ref, weight_ref, parents_ref, length_ref, group_ref, arrival
):
    requests, node_count = parents_ref.shape
    touched, slot_count = suffix_ref.shape[:2]
    start = pl.multiple_of(first_row(chunk_rows, 2), math.gcd(chunk_rows, node_count))
    pair_start = pl.multiple_of(first_row(chunk_rows, 3), math.gcd(chunk_rows, node_count))
    base = first_request(chunk_rows, 2, node_count, requests, touched)
    copies = [
        pltpu.make_async_copy(source, target, arrival.at[place])
        for place, (source, target) in enumerate((
            (parents_hbm, parents_ref),
            (length_hbm, length_ref),
            (group_hbm, group_ref),
            (own_hbm.at[pl.ds(start, chunk_rows)], own_ref),
            (own_hbm.at[pl.ds(pair_start, chunk_rows)], pair_ref),
            (tree_hbm.at[pl.ds(pl.multiple_of(base * node_count, node_count), touched * node_count)], tree_ref),
            (suffix_hbm.at[pl.ds(base, touched)], suffix_ref),
            (shard_hbm, shard_ref),
            (weight_hbm, weight_ref),
        ))
    ]
    for copy in copies:
        copy.start()
    for copy in copies[:3]:
        copy.wait()
    found = closures([parents_ref[pl.ds(base + k, 1), :] for k in range(touched)], node_count)
    slot = lax.broadcasted_iota(jnp.int32, (1, slot_count), 1)
    for k in range(touched):
        bias_ref[k * node_count : (k + 1) * node_count, :] = bias_of(found[k])
        notes_ref[k, :1, :] = jnp.where(slot < length_ref[base + k], 0.0, neg_large)
        notes_ref[k, 1:2, :] = jnp.broadcast_to(group_ref[base + k].astype(jnp.float32), (1, slot_count))
    for copy in copies[3:]:
        copy.wait()


def private_kernel(unit, chunk_rows, node_count, requests, bias_ref, notes_ref, own_ref, tree_ref, suffix_ref, other_ref, *rest):
    head_size = tree_ref.shape[1] // 2
    touched = suffix_ref.shape[0]
    *parts, state_ref = rest
    prompts = kept_prompts(*parts) if parts else []
    start = pl.multiple_of(first_row(chunk_rows, 2), unit)
    base = first_request(chunk_rows, 2, node_count, requests, touched)
    for number in range(chunk_rows // unit):
        row = pl.multiple_of(start + number * unit, unit)
        place = row // node_count - base
        query = jnp.concatenate(
            [stacked_heads(own_ref, number * unit, unit, head_size), stacked_heads(other_ref, number * unit, unit, head_size)], axis=0
        )
        bias = bias_ref[pl.ds(pl.multiple_of(row - base * node_count, unit), unit), :]
        tree = tree_ref[pl.ds(pl.multiple_of(place * node_count, node_count), node_count), :]
        notes = notes_ref[place]
        group = notes[1:2]
        blocks = private_blocks(query, bias, notes[:1], tree, suffix_ref[place])
        if prompts:
            prompt = prompt_of(prompts, group[:, : 2 * head_size])
            blocks.append((score(query, prompt[:, :head_size]), prompt[:, head_size:]))
        largest, total, result = absorb(blocks, log2_rate(head_size))
        lanes = result.shape
        rows = slice(number * lanes[0], (number + 1) * lanes[0])
        for spot, value in enumerate((result, largest, total, group[:, :head_size])):
            state_ref[rows, spot * head_size : (spot + 1) * head_size] = jnp.broadcast_to(value, lanes)


def in_smem():
    return pl.BlockSpec(memory_space=pltpu.SMEM)


def in_vmem():
    return pl.BlockSpec(memory_space=pltpu.VMEM)


def load(unit, chunk_rows, parents, lengths, groups, own, tree_kv, suffix_kv, shard, weight):
    requests, node_count = parents.shape
    touched = min(requests, -(-(chunk_rows + node_count - unit) // node_count))
    sources = [pltpu.with_memory_space_constraint(a, pltpu.HBM) for a in (parents, lengths, groups, own, tree_kv, suffix_kv, shard, weight)]
    return pl.pallas_call(
        functools.partial(load_kernel, chunk_rows),
        in_specs=[pl.BlockSpec(memory_space=pltpu.HBM)] * 8,
        out_specs=[in_vmem()] * 8,
        out_shape=(
            jax.ShapeDtypeStruct((touched * node_count, node_count), jnp.float32),
            jax.ShapeDtypeStruct((touched, 8, suffix_kv.shape[1]), jnp.float32),
            jax.ShapeDtypeStruct((chunk_rows, own.shape[1]), own.dtype),
            jax.ShapeDtypeStruct((touched * node_count, tree_kv.shape[1]), tree_kv.dtype),
            jax.ShapeDtypeStruct((touched, *suffix_kv.shape[1:]), suffix_kv.dtype),
            jax.ShapeDtypeStruct((chunk_rows, own.shape[1]), own.dtype),
            jax.ShapeDtypeStruct(shard.shape, shard.dtype),
            jax.ShapeDtypeStruct(weight.shape, weight.dtype),
        ),
        scratch_shapes=[
            pltpu.VMEM(parents.shape, jnp.int32),
            pltpu.SMEM(lengths.shape, jnp.int32),
            pltpu.SMEM(groups.shape, jnp.int32),
            pltpu.SemaphoreType.DMA((9,)),
        ],
        compiler_params=pltpu.CompilerParams(vmem_limit_bytes=vmem_bytes),
        name="load",
        cost_estimate=pl.CostEstimate(flops=100_000_000, bytes_accessed=2_000_000, transcendentals=0),
    )(*sources)


def private(unit, chunk_rows, node_count, requests, loaded, other, parts):
    bias, notes, own, tree, suffix = loaded
    head_size = tree.shape[1] // 2
    state_rows = chunk_rows * 2 * (own.shape[1] // head_size)
    return pl.pallas_call(
        functools.partial(private_kernel, unit, chunk_rows, node_count, requests),
        in_specs=[in_vmem()] * (6 + len(parts)),
        out_specs=in_vmem(),
        out_shape=jax.ShapeDtypeStruct((state_rows, 4 * head_size), jnp.float32),
        compiler_params=pltpu.CompilerParams(vmem_limit_bytes=vmem_bytes),
        name="private",
        cost_estimate=pl.CostEstimate(flops=300_000_000, bytes_accessed=500_000, transcendentals=0),
    )(*loaded, other, *parts)


def far_kernel(unit, part_count, own_ref, other_ref, state_ref, *rest):
    parts, (weight_own_ref, weight_other_ref, out_ref, attended_ref) = rest[:part_count], rest[part_count:]
    chunk_rows = out_ref.shape[0]
    head_size = state_ref.shape[1] // 4
    rate = log2_rate(head_size)
    prompts = swapped_prompts(parts[0], parts[1], parts[0].shape[0] // fetches) if part_count == 2 else [parts[0][g] for g in range(parts[0].shape[0])]
    start = first_row(chunk_rows, 2)
    for number in range(chunk_rows // unit):
        row = pl.multiple_of(start + number * unit, unit)
        query = jnp.concatenate(
            [stacked_heads(own_ref, number * unit, unit, head_size), stacked_heads(other_ref, number * unit, unit, head_size)], axis=0
        )
        rows = slice(number * query.shape[0], (number + 1) * query.shape[0])
        before, largest, total, group = (state_ref[rows, spot * head_size : (spot + 1) * head_size] for spot in range(4))
        prompt = prompt_of(prompts, jnp.concatenate([group[:1], group[:1]], axis=1))
        scores = score(query, prompt[:, :head_size])
        top = jnp.maximum(largest, jnp.max(scores, axis=1, keepdims=True))
        fade = jnp.exp2((largest - top) * rate)
        width = scores.shape[1] // head_size
        weight = jnp.exp2((scores - (top if width == 1 else jnp.concatenate([top] * width, axis=1))) * rate)
        total = total * fade + jnp.sum(weight, axis=1, keepdims=True)
        result = before * fade + jnp.dot(weight.astype(jnp.bfloat16), prompt[:, head_size:], preferred_element_type=jnp.float32)
        put_heads(attended_ref, number, unit, (result / total).astype(jnp.bfloat16))
    project(attended_ref, weight_own_ref, weight_other_ref, out_ref)


def near_kernel(
    unit, piece_count, length_ref, group_ref, own_ref, other_ref, parents_ref, accepted_ref, tree_ref, suffix_ref, *rest
):
    pieces, (weight_own_ref, weight_other_ref, out_ref, path_ref, attended_ref, bias_ref) = rest[:piece_count], rest[piece_count:]
    chunk_rows = out_ref.shape[0]
    requests, node_count = parents_ref.shape
    path_length = accepted_ref.shape[1]
    head_size = tree_ref.shape[1] // 2
    node = lax.broadcasted_iota(jnp.int32, (node_count, path_length), 0)
    for r, closure in enumerate(closures([parents_ref[r : r + 1, :] for r in range(requests)], node_count)):
        rows = slice(r * node_count, (r + 1) * node_count)
        bias_ref[rows, :] = bias_of(closure)
        chosen = jnp.broadcast_to(accepted_ref[r : r + 1, :], (node_count, path_length)) == node
        path_ref[r] = lax.dot_general(
            jnp.where(chosen, 1.0, 0.0).astype(jnp.bfloat16),
            tree_ref[rows, :],
            (((0,), (0,)), ((), ())),
            preferred_element_type=jnp.float32,
        ).astype(jnp.bfloat16)
    if piece_count == 3:
        kept = kept_prompts(pieces[0], pieces[1])
        prompts = [jnp.concatenate(pair, axis=0) for pair in zip(kept, swapped_prompts(pieces[1], pieces[2], len(kept)))]
    else:
        prompts = [pieces[0][g] for g in range(pieces[0].shape[0])]
    slot = lax.broadcasted_iota(jnp.int32, (1, suffix_ref.shape[1]), 1)
    start = first_row(chunk_rows, 0)
    for number in range(chunk_rows // unit):
        row = pl.multiple_of(start + number * unit, unit)
        query = jnp.concatenate([stacked_heads(ref, row, unit, head_size) for ref in (own_ref, other_ref)], axis=0)
        request = row // node_count
        used = jnp.where(slot < length_ref[request], 0.0, neg_large)
        tree = tree_ref[pl.ds(pl.multiple_of(request * node_count, node_count), node_count), :]
        blocks = private_blocks(query, bias_ref[pl.ds(row, unit), :], used, tree, suffix_ref[request])
        group = group_ref[request]
        prompt = prompt_of(prompts, group)
        blocks.append((score(query, prompt[:, :head_size]), prompt[:, head_size:]))
        largest, total, result = absorb(blocks, log2_rate(head_size))
        put_heads(attended_ref, number, unit, (result / total).astype(jnp.bfloat16))
    project(attended_ref, weight_own_ref, weight_other_ref, out_ref)


def chunk(kernel, name, outs, scalars, arrays, weights, scratch=(), flops=500_000_000):
    return pl.pallas_call(
        kernel,
        in_specs=[in_smem()] * len(scalars) + [in_vmem()] * (len(arrays) + len(weights)),
        out_specs=[in_vmem()] * len(outs),
        out_shape=outs,
        scratch_shapes=scratch,
        compiler_params=pltpu.CompilerParams(vmem_limit_bytes=vmem_bytes),
        name=name,
        cost_estimate=pl.CostEstimate(flops=flops, bytes_accessed=1_000_000, transcendentals=0),
    )(*scalars, *arrays, *weights)


def local(req_count, tp_count, queries, tree_kv, suffix_kv, suffix_len, group_ids, parents, accepted, prompt_kv, out_weight):
    chunk_rows = queries.shape[0] // tp_count
    unit = math.gcd(chunk_rows, parents.shape[1])
    if req_count == 8 and tp_count % 2 == 0:
        fetched = fetch_shards(prompt_kv, req_count, tp_count)
        other_weight = swap_in_pair(out_weight, tp_count)
    else:
        fetched = None
        other_weight = swap_in_pair(out_weight, tp_count)
    requests, node_count = parents.shape
    *loaded, pair_queries, shard, own_weight = load(unit, chunk_rows, parents, suffix_len, group_ids, queries, tree_kv, suffix_kv, prompt_kv, out_weight)
    far_queries = touched(swap_in_pair(pair_queries, tp_count))
    if fetched is None:
        pieces = [lax.all_gather(prompt_kv, "req", axis=1, tiled=True)]
        state = private(unit, chunk_rows, node_count, requests, loaded, far_queries, [])
    else:
        joined = jnp.concatenate([after(piece, shard) for piece in fetched], axis=0)
        pieces = [shard, joined, swap_in_pair(joined, tp_count)]
        state = private(unit, chunk_rows, node_count, requests, loaded, far_queries, pieces[:2])
    parts = pieces[-2:]
    weights = (own_weight, other_weight)
    columns = out_weight.shape[1]
    early = columns // 4
    attended_shape = (chunk_rows, 2 * out_weight.shape[0])
    early_far, attended = chunk(
        functools.partial(far_kernel, unit, len(parts)), "far_chunk",
        [jax.ShapeDtypeStruct((chunk_rows, early), jnp.bfloat16), jax.ShapeDtypeStruct(attended_shape, jnp.bfloat16)],
        (), (loaded[2], far_queries, state, *parts), weights, flops=200_000_000
    )
    across = [(t, t ^ 2) for t in range(tp_count)]
    early_arrived = touched(lax.ppermute(early_far, "tp", across))
    (late_far,) = chunk(
        functools.partial(rest_kernel, early), "far_rest", [jax.ShapeDtypeStruct((chunk_rows, columns - early), jnp.bfloat16)],
        (), (attended,), weights, flops=300_000_000
    )
    late_arrived = lax.ppermute(late_far, "tp", across)
    other_queries = swap_in_pair(after(queries, late_far), tp_count)
    near, path_cache = chunk(
        functools.partial(near_kernel, unit, len(pieces)), "near_chunk",
        [jax.ShapeDtypeStruct((chunk_rows, columns), jnp.float32), jax.ShapeDtypeStruct((*accepted.shape, tree_kv.shape[1]), jnp.bfloat16)],
        (suffix_len, group_ids), (queries, other_queries, parents, accepted, tree_kv, suffix_kv, *pieces), weights,
        (pltpu.VMEM(attended_shape, jnp.bfloat16), pltpu.VMEM((requests * node_count, node_count), jnp.float32))
    )
    (layer_output,) = chunk(
        sum_kernel, "sum", [jax.ShapeDtypeStruct((chunk_rows, columns), jnp.bfloat16)], (), (near, early_arrived, late_arrived), (), flops=1_000_000
    )
    return (layer_output, path_cache)


def solution(mesh):
    return jax.shard_map(
        functools.partial(local, mesh.shape["req"], mesh.shape["tp"]),
        mesh=mesh,
        in_specs=(
            P("req", "tp"),
            P("req", None),
            P("req", None, None),
            P("req"),
            P("req"),
            P("req", None),
            P("req", None),
            P(None, "req", None),
            P("tp", None),
        ),
        out_specs=(P(("req", "tp"), None), P("req", None, None)),
        check_vma=False,
    )
```
